128 devices in a mesh: dp: 2 (over z_hi), expert: 64 (over z_lo, y, x, core).
Axes of the slice: x: 4, y: 4, z: 4 (z_hi: 2, z_lo: 2; z = z_hi * 2 + z_lo), core: 2. Of those that a mesh axis runs over, the one named last changes fastest.
Arguments:
- tokens: bfloat16 [8192, 3584], P(('dp', 'expert')), may hold values from -6 to 6
- expert_ids: int32 [8192, 8], P(('dp', 'expert')), may hold values from 0 to 63, all different within a row; in each aligned block of 64 rows (0 to 63, 64 to 127, ...) at most 16 rows name the same one
- router_weight: bfloat16 [3584, 64], replicated, may hold values from -0.09375 to 0.09375
- gate_weight: bfloat16 [64, 3584, 1024], P('expert'), may hold values from -0.09375 to 0.09375
- up_weight: bfloat16 [64, 3584, 1024], P('expert'), may hold values from -0.09375 to 0.09375
- down_weight: bfloat16 [64, 1024, 3584], P('expert'), may hold values from -0.1875 to 0.1875
Outputs:
- mixed: bfloat16 [8192, 3584], P(('dp', 'expert'))
- load_ratio: float32 [64], replicated
The draws below stay inside these ranges and needn't reach their ends.
Inputs may be any that keep to these rules, and one draw needn't show every extreme that they name: `expert_ids`: each row names 8 different experts; among the rows of one device no expert is named by more than 16 rows, a bound that some block reaches.
All inputs are finite; a program needn't handle non-finite values.
Results may differ from the reference program's by a relative error of at most 0.0058.
Values may be sent and summed in bfloat16 or wider, within the bound.
A program may use at most 192 MiB of HBM per device.

```python
import math
import jax
import jax.numpy as jnp
import numpy as np
from jax import lax

D = 3584
F = 1024
TOPK = 8
TOK_DEV = 64
EXPERTS = 64
TOKENS = 8192
CAP = 16


def block_scale(rng, dims, shards, least, top_value):
    loudness = 1.0
    for position, parts in shards:
        heights = jax.random.uniform(jax.random.fold_in(jax.random.fold_in(rng, 6), position), (parts,), jnp.float32, least / len(shards), top_value / len(shards))
        loudness = loudness * jnp.repeat(jnp.exp(heights), dims[position] // parts).reshape((-1,) + (1,) * (len(dims) - 1 - position))
    return loudness


def routed_block(stream_key, own, number, rows, count, top, reach, lean):
    sequence = jax.random.permutation(stream_key, count)
    heavy_load, common = portions_of(count, rows * top, reach, lean, True), portions_of(count, rows * top, reach, lean, False)
    places = jnp.arange(count)

    def named(tallies, turn):
        used = int((tallies > 0).sum())
        fixed = max(1, used // 4)
        passed = fixed + (places - fixed + turn * (used - fixed)) % max(1, count - fixed)
        return jnp.zeros((count,), jnp.int32).at[sequence[jnp.where(places < fixed, places, passed)]].set(jnp.asarray(tallies, jnp.int32))

    tallies = jnp.where(number % 4 == 0, named(heavy_load, number // 4), named(common, number - number // 4 - 1))
    mixed = jax.random.permutation(jax.random.fold_in(own, 3), count)
    donor, receiver = mixed[0:count // 2 * 2:2], mixed[1:count // 2 * 2:2]
    margin = jnp.minimum(tallies[donor] - 1, reach - tallies[receiver]) // 2
    margin = jnp.where((donor == sequence[0]) | (receiver == sequence[0]) | (tallies[receiver] == 0), 0, jnp.maximum(margin, 0))
    passed = jax.random.randint(jax.random.fold_in(own, 4), (count // 2,), 0, 1 << 20) % (margin + 1)
    tallies = tallies.at[donor].add(-passed).at[receiver].add(passed)
    members = jnp.searchsorted(jnp.cumsum(tallies), jnp.arange(rows * top), side="right").astype(jnp.int32)
    listing = members.reshape(top, rows).T
    listing = listing[jax.random.permutation(jax.random.fold_in(own, 1), rows)]
    turn = jax.random.randint(jax.random.fold_in(own, 2), (rows, 1), 0, top)
    return jnp.take_along_axis(listing, (jnp.arange(top)[None, :] + turn) % top, axis=1)


def portions_of(count, total, most, slope, full):
    weights = [(1 << 20) // math.isqrt(grade ** slope) + 1 for grade in range(1, count + 1)]
    largest = most if full else min(most, max(-(-total // count), total * weights[0] // sum(weights)))
    least = 1 if total - largest >= count - 1 else 0
    counts, spare = [largest] + [least] * (count - 1), total - largest - least * (count - 1)
    while spare > 0:
        free = [i for i in range(1, count) if counts[i] < largest] or [i for i in range(1, count) if counts[i] < most]
        pool, left = sum([weights[i] for i in free]), spare
        for i in free:
            extra = min(most - counts[i], max(1, left * weights[i] // pool), spare)
            counts[i] = counts[i] + extra
            spare = spare - extra
    return np.array(counts)


def scatter_about(own_key, extent, scale, reach, shards=(), kind=jnp.bfloat16):
    result = scale * jax.random.normal(own_key, extent, jnp.float32)
    if shards:
        result = result * block_scale(own_key, extent, shards, -0.22, 0.18)
    return jnp.clip(result, -reach, reach).astype(kind)


def setup_inputs(seed: int = 0) -> dict:
    key_of = jax.random.split(jax.random.key(seed), 7)
    tokens = scatter_about(key_of[0], (TOKENS, D), 1.0, 6.0, ((0, 128),))
    expert_ids_keys = jax.random.split(jax.random.fold_in(key_of[1], 1), TOKENS // TOK_DEV)
    expert_ids_turns = jax.random.permutation(jax.random.fold_in(key_of[1], 3), TOKENS // TOK_DEV)
    expert_ids = jax.vmap(lambda own, number: routed_block(jax.random.fold_in(key_of[1], 2), own, number, TOK_DEV, EXPERTS, TOPK, CAP, 2))(expert_ids_keys, expert_ids_turns).reshape((TOKENS, TOPK))
    router_weight = scatter_about(key_of[2], (D, EXPERTS), D ** -0.5, 0.09375)
    gate_weight = scatter_about(key_of[3], (EXPERTS, D, F), D ** -0.5, 0.09375, ((0, 64),))
    up_weight = scatter_about(key_of[4], (EXPERTS, D, F), D ** -0.5, 0.09375, ((0, 64),))
    down_weight = scatter_about(key_of[5], (EXPERTS, F, D), F ** -0.5, 0.1875, ((0, 64),))
    return {"tokens": tokens, "expert_ids": expert_ids, "router_weight": router_weight, "gate_weight": gate_weight, "up_weight": up_weight, "down_weight": down_weight}


def expert_swiglu(inputs, gate_matrix, up_matrix, down_matrix):
    gate_part = jnp.dot(inputs, gate_matrix, preferred_element_type=jnp.float32)
    up_part = jnp.dot(inputs, up_matrix, preferred_element_type=jnp.float32)
    hidden = (jax.nn.silu(gate_part) * up_part).astype(jnp.bfloat16)
    return jnp.dot(hidden, down_matrix, preferred_element_type=jnp.float32).astype(jnp.bfloat16)


def reference(tokens, expert_ids, router_weight, gate_weight, up_weight, down_weight):
    logits = jnp.dot(tokens, router_weight, preferred_element_type=jnp.float32)
    affinity = jax.nn.sigmoid(jnp.take_along_axis(logits, expert_ids, axis=1))
    gate_values = 2.5 * affinity / jnp.sum(affinity, axis=1, keepdims=True)
    pair_total = TOKENS * TOPK
    pair_expert = expert_ids.reshape(-1).astype(jnp.int32)
    expert_range = jnp.arange(EXPERTS, dtype=jnp.int32)
    expert_loads = jnp.sum((pair_expert[:, None] == expert_range[None, :]).astype(jnp.int32), axis=0)
    tile_rows = 32
    sort_order = jnp.argsort(pair_expert, stable=True).astype(jnp.int32)
    sorted_expert = pair_expert[sort_order]
    padded = ((expert_loads + tile_rows - 1) // tile_rows * tile_rows).astype(jnp.int32)
    padded_start = (jnp.cumsum(padded) - padded).astype(jnp.int32)
    plain_start = (jnp.cumsum(expert_loads) - expert_loads).astype(jnp.int32)
    positions = jnp.arange(pair_total, dtype=jnp.int32)
    slot_of_sorted = (padded_start[sorted_expert] + positions - plain_start[sorted_expert]).astype(jnp.int32)
    tile_total = pair_total // tile_rows + EXPERTS + 1
    source_pair = jnp.full((tile_total * tile_rows,), pair_total, jnp.int32).at[slot_of_sorted].set(sort_order)
    tile_start = jnp.arange(tile_total, dtype=jnp.int32) * tile_rows
    tile_expert = jnp.minimum(jnp.sum(((padded_start + padded)[None, :] <= tile_start[:, None]).astype(jnp.int32), axis=1), EXPERTS - 1).astype(jnp.int32)
    padded_tokens = jnp.concatenate([tokens, jnp.zeros((1, D), tokens.dtype)], axis=0)
    source_token = jnp.minimum(source_pair // TOPK, TOKENS).astype(jnp.int32)

    def one_tile(tile_args):
        token_rows, tile_which = tile_args
        tile_block = padded_tokens[token_rows]
        return expert_swiglu(tile_block, gate_weight[tile_which], up_weight[tile_which], down_weight[tile_which])

    outputs = lax.map(one_tile, (source_token.reshape(tile_total, tile_rows), tile_expert))
    pair_outputs = jnp.zeros((pair_total + 1, D), outputs.dtype).at[source_pair].set(outputs.reshape(tile_total * tile_rows, D))
    weighted = gate_values[:, :, None] * pair_outputs[:pair_total].reshape(TOKENS, TOPK, D).astype(jnp.float32)
    mixed = jnp.sum(weighted, axis=1).astype(jnp.bfloat16)
    load_ratio = expert_loads.astype(jnp.float32) * EXPERTS / (TOKENS * TOPK)
    return mixed, load_ratio
```

```python
import functools

import jax
import jax.numpy as jnp
from jax import lax
from jax.experimental import pallas as pl
from jax.experimental.pallas import tpu as pltpu
from jax.sharding import PartitionSpec as P

MESH = pl.DeviceIdType.MESH
CAP = 16
NEAR = 8


def moe_kernel(
    sizes,
    tokens_ref, ids_ref, router_ref, wg_hbm, wu_hbm, wd_hbm,
    mixed_ref, load_ref,
    wg, wu, wd, gathered, routes, packed, served, back, sums, hidden, route, tally, tallies, twin,
    w_sem, g_send, g_recv, r_send, r_recv, d_send, d_recv, t_send, t_recv, p_send, p_recv,
    c_send, c_recv, x_send, x_recv,
):
    rows, depth, width, experts, top = sizes
    f32, bf16 = jnp.float32, jnp.bfloat16
    dp, me = lax.axis_index("dp"), lax.axis_index("expert")
    c = me % 2
    x = (me // 2) % 4
    y = (me // 8) % 4
    z = me // 32
    g = (1 - c) * y + c * x
    h = (1 - c) * x + c * y
    g_step, h_step = 8 - 6 * c, 2 + 6 * c
    my_place = h * 2 + c
    my_source = c * 4 + h
    slot_rows = 2 * CAP

    def offset_of(m):
        return m + (m // 2) * (1 - 2 * (m % 2))

    def chunk_there(m):
        return (m % 2) * 2 + m // 2

    def plane_device(m, q):
        return (z + q - 2 * z * q) * 32 + ((g + offset_of(m)) % 4) * g_step + h * h_step + c

    def served_device(place):
        return z * 32 + g * g_step + (place // 2) * h_step + place % 2

    def source_device(source):
        kind, far = source // 4, source % 4
        return z * 32 + (1 - kind) * (y * 8 + far * 2) + kind * (far * 8 + x * 2 + 1)

    def place_there(source):
        kind = source // 4
        return ((1 - kind) * x + kind * y) * 2 + c

    def rows_of(index):
        return pl.ds(pl.multiple_of(index * slot_rows, slot_rows), slot_rows)

    barrier = pltpu.get_barrier_semaphore()

    def greet(device):
        pl.semaphore_signal(barrier, inc=1, device_id=device, device_id_type=MESH)

    for i in range(1, NEAR):
        greet((dp, plane_device(i // 2, i % 2)))

    def greet_sets(k, carry):
        greet((dp, served_device((my_place + k) % NEAR)))
        greet((dp, source_device((my_source + k) % NEAR)))
        return carry

    lax.fori_loop(1, NEAR, greet_sets, 0)
    greet((1 - dp, me))

    weights = [
        pltpu.make_async_copy(wg_hbm.at[0], wg, w_sem.at[0]),
        pltpu.make_async_copy(wu_hbm.at[0], wu, w_sem.at[1]),
        pltpu.make_async_copy(wd_hbm.at[0], wd, w_sem.at[2]),
    ]
    for copy in weights:
        copy.start()

    token_block = tokens_ref[...]
    logits = jnp.dot(token_block, router_ref[...], preferred_element_type=f32)
    lane = lax.broadcasted_iota(jnp.int32, (rows, experts), 1)
    chosen = jnp.zeros((rows, experts), f32)
    for k in range(top):
        chosen = jnp.where(ids_ref[:, k : k + 1] == lane, 1.0, chosen)
    affinity = jnp.where(chosen > 0, 1.0 / (1.0 + jnp.exp(-logits)), 0.0)
    gates = 2.5 * affinity / jnp.sum(affinity, axis=1, keepdims=True)
    later = lax.broadcasted_iota(jnp.int32, (rows, rows), 0)
    earlier = lax.broadcasted_iota(jnp.int32, (rows, rows), 1)
    upto = jnp.where(earlier <= later, 1.0, 0.0).astype(bf16)
    ranks = jnp.dot(upto, chosen.astype(bf16), preferred_element_type=f32)
    both = jnp.concatenate([chosen * ranks, gates], axis=1)
    route[...] = jnp.concatenate([both, both], axis=0).T
    gathered[0, 0:rows, :] = token_block
    routes[0, 0] = route[...]

    pl.semaphore_wait(barrier, 3 * (NEAR - 1) + 1)

    def token_copy(i):
        m, q = i // 2, i % 2
        slot = chunk_there(m)
        return pltpu.make_async_remote_copy(
            src_ref=tokens_ref,
            dst_ref=gathered.at[slot, pl.ds(q * rows, rows)],
            send_sem=g_send.at[i],
            recv_sem=g_recv.at[slot * 2 + q],
            device_id=(dp, plane_device(m, q)),
            device_id_type=MESH,
        )

    def route_copy(i):
        m, q = i // 2, i % 2
        slot = chunk_there(m)
        return pltpu.make_async_remote_copy(
            src_ref=route,
            dst_ref=routes.at[slot, q],
            send_sem=r_send.at[i],
            recv_sem=r_recv.at[slot * 2 + q],
            device_id=(dp, plane_device(m, q)),
            device_id_type=MESH,
        )

    for i in range(1, NEAR):
        token_copy(i).start()
        route_copy(i).start()

    def landed(ref, sem):
        pltpu.make_async_copy(ref, ref, sem).wait()

    def wait_block(m, q):
        landed(gathered.at[m, pl.ds(q * rows, rows)], g_recv.at[m * 2 + q])
        landed(routes.at[m, q], r_recv.at[m * 2 + q])

    def spread(m, base):
        first_half = lax.broadcasted_iota(jnp.int32, (1, 2 * rows), 1) < rows
        bands = []
        for place in range(NEAR):
            expert = base + served_device(place)
            row = jnp.where(
                first_half, routes[m, 0, pl.ds(expert, 1), :], routes[m, 1, pl.ds(expert, 1), :]
            )
            bands.append(jnp.broadcast_to(row, (slot_rows, 2 * rows)))
        return jnp.concatenate(bands, axis=0)

    def taken(m):
        slot = lax.broadcasted_iota(jnp.int32, (NEAR * slot_rows, 2 * rows), 0) % slot_rows
        block = lax.broadcasted_iota(jnp.int32, (NEAR * slot_rows, 2 * rows), 1) // rows
        wanted = jnp.where(slot // CAP == block, slot % CAP + 1, -1).astype(f32)
        return spread(m, 0) == wanted

    def pack_chunk(m):
        select = jnp.where(taken(m), 1.0, 0.0).astype(bf16)

        def tile(n, carry):
            columns = pl.ds(pl.multiple_of(n * 512, 512), 512)
            packed[m, :, columns] = jnp.dot(
                select, gathered[m, :, columns], preferred_element_type=f32
            ).astype(bf16)
            return carry

        lax.fori_loop(0, depth // 512, tile, 0)

    def hand_out(m, k):
        place = (my_place + k) % NEAR
        return pltpu.make_async_remote_copy(
            src_ref=packed.at[m, rows_of(place)],
            dst_ref=served.at[m, rows_of(my_source)],
            send_sem=d_send.at[m * NEAR + k],
            recv_sem=d_recv.at[m * NEAR + my_source],
            device_id=(dp, served_device(place)),
            device_id_type=MESH,
        )

    def pack_and_send(m, carry):
        @pl.when(m > 0)
        def _():
            wait_block(m, 0)

        wait_block(m, 1)
        pack_chunk(m)

        def send(k, carry):
            hand_out(m, k).start()
            return carry

        lax.fori_loop(1, NEAR, send, 0)
        pltpu.make_async_copy(
            packed.at[m, rows_of(my_place)],
            served.at[m, rows_of(my_source)],
            d_recv.at[m * NEAR + my_source],
        ).start()
        return carry

    lax.fori_loop(0, 4, pack_and_send, 0)

    plane = jnp.zeros((experts, 2 * rows), f32)
    for i in range(NEAR):
        plane = plane + jnp.where(routes[i // 2, i % 2, 0:experts, :] > 0, 0.5, 0.0)
    tally[...] = plane

    def tally_copy(k):
        return pltpu.make_async_remote_copy(
            src_ref=tally,
            dst_ref=tallies.at[my_source],
            send_sem=c_send.at[k],
            recv_sem=c_recv.at[my_source],
            device_id=(dp, served_device((my_place + k) % NEAR)),
            device_id_type=MESH,
        )

    def send_tally(k, carry):
        tally_copy(k).start()
        return carry

    lax.fori_loop(1, NEAR, send_tally, 0)
    pltpu.make_async_copy(tally, tallies.at[my_source], c_recv.at[my_source]).start()

    for copy in weights:
        copy.wait()

    def hand_back(m, k):
        source = (my_source + k) % NEAR
        place = place_there(source)
        return pltpu.make_async_remote_copy(
            src_ref=served.at[m, rows_of(source)],
            dst_ref=back.at[m, rows_of(place)],
            send_sem=t_send.at[m * NEAR + k],
            recv_sem=t_recv.at[m * NEAR + place],
            device_id=(dp, source_device(source)),
            device_id_type=MESH,
        )

    def serve(m, carry):
        def arrive(source, carry):
            landed(served.at[m, rows_of(source)], d_recv.at[m * NEAR + source])
            return carry

        lax.fori_loop(0, NEAR, arrive, 0)

        def into_hidden(n, carry):
            columns = pl.ds(pl.multiple_of(n * 256, 256), 256)
            gate_part = jnp.dot(served[m], wg[:, columns], preferred_element_type=f32)
            up_part = jnp.dot(served[m], wu[:, columns], preferred_element_type=f32)
            act = gate_part / (1.0 + jnp.exp(-gate_part)) * up_part
            hidden[:, columns] = act.astype(bf16)
            return carry

        lax.fori_loop(0, width // 256, into_hidden, 0)

        def out_of_hidden(n, carry):
            columns = pl.ds(pl.multiple_of(n * 512, 512), 512)
            served[m, :, columns] = jnp.dot(
                hidden[...], wd[:, columns], preferred_element_type=f32
            ).astype(bf16)
            return carry

        lax.fori_loop(0, depth // 512, out_of_hidden, 0)

        def send(k, carry):
            hand_back(m, k).start()
            return carry

        lax.fori_loop(1, NEAR, send, 0)
        pltpu.make_async_copy(
            served.at[m, rows_of(my_source)],
            back.at[m, rows_of(my_place)],
            t_recv.at[m * NEAR + my_place],
        ).start()
        return carry

    lax.fori_loop(0, 4, serve, 0)

    group = jnp.zeros((experts, 2 * rows), f32)
    for source in range(NEAR):
        landed(tallies.at[source], c_recv.at[source])
        group = group + tallies[source]
    twin[0] = group
    twin_copy = pltpu.make_async_remote_copy(
        src_ref=twin.at[0],
        dst_ref=twin.at[1],
        send_sem=x_send,
        recv_sem=x_recv,
        device_id=(1 - dp, me),
        device_id_type=MESH,
    )
    twin_copy.start()

    def sum_copy(m, q):
        slot = chunk_there(m)
        return pltpu.make_async_remote_copy(
            src_ref=gathered.at[m, pl.ds(q * rows, rows)],
            dst_ref=sums.at[slot * 2 + q],
            send_sem=p_send.at[m * 2 + q],
            recv_sem=p_recv.at[slot * 2 + q],
            device_id=(dp, plane_device(m, q)),
            device_id_type=MESH,
        )

    def combine(m, carry):
        def arrive(place, carry):
            landed(back.at[m, rows_of(place)], t_recv.at[m * NEAR + place])
            return carry

        lax.fori_loop(0, NEAR, arrive, 0)
        weight = jnp.where(taken(m), spread(m, experts), 0.0).T
        high = weight.astype(bf16)
        low = (weight - high.astype(f32)).astype(bf16)

        def tile(n, carry):
            columns = pl.ds(pl.multiple_of(n * 512, 512), 512)
            block = back[m, :, columns]
            total = jnp.dot(high, block, preferred_element_type=f32)
            total = total + jnp.dot(low, block, preferred_element_type=f32)
            gathered[m, :, columns] = total.astype(bf16)
            return carry

        lax.fori_loop(0, depth // 512, tile, 0)

        @pl.when(m > 0)
        def _():
            sum_copy(m, 0).start()

        sum_copy(m, 1).start()
        return carry

    lax.fori_loop(0, 4, combine, 0)

    twin_copy.wait()
    pairs = (twin[0] + twin[1]) * (1.0 / 1024.0)
    load_ref[...] = jnp.sum(
        jnp.concatenate([pairs, jnp.zeros_like(pairs)], axis=0).T, axis=0, keepdims=True
    )

    for i in range(1, NEAR):
        landed(sums.at[i], p_recv.at[i])

    def finish(n, carry):
        columns = pl.ds(pl.multiple_of(n * 512, 512), 512)
        total = gathered[0, 0:rows, columns].astype(f32)
        for i in range(1, NEAR):
            total = total + sums[i, :, columns].astype(f32)
        mixed_ref[:, columns] = total.astype(bf16)
        return carry

    lax.fori_loop(0, depth // 512, finish, 0)

    for i in range(1, NEAR):
        token_copy(i).wait_send()
        route_copy(i).wait_send()
        sum_copy(i // 2, i % 2).wait_send()

    def sent(k, carry):
        tally_copy(k).wait_send()

        def sent_chunk(m, carry):
            hand_out(m, k).wait_send()
            hand_back(m, k).wait_send()
            return carry

        return lax.fori_loop(0, 4, sent_chunk, carry)

    lax.fori_loop(1, NEAR, sent, 0)


def local(tokens, expert_ids, router_weight, gate_weight, up_weight, down_weight):
    rows, depth = tokens.shape
    top = expert_ids.shape[1]
    experts = router_weight.shape[1]
    width = gate_weight.shape[2]
    bf16, f32 = jnp.bfloat16, jnp.float32
    slots = NEAR * 2 * CAP
    vmem = pl.BlockSpec(memory_space=pltpu.VMEM)
    hbm = pl.BlockSpec(memory_space=pl.ANY)
    dma = pltpu.SemaphoreType.DMA
    mixed, load = pl.pallas_call(
        functools.partial(moe_kernel, (rows, depth, width, experts, top)),
        out_shape=(
            jax.ShapeDtypeStruct((rows, depth), bf16),
            jax.ShapeDtypeStruct((1, 2 * experts), f32),
        ),
        in_specs=[vmem, vmem, vmem, hbm, hbm, hbm],
        out_specs=(vmem, vmem),
        scratch_shapes=[
            pltpu.VMEM((depth, width), bf16),
            pltpu.VMEM((depth, width), bf16),
            pltpu.VMEM((width, depth), bf16),
            pltpu.VMEM((4, 2 * rows, depth), bf16),
            pltpu.VMEM((4, 2, 2 * experts, 2 * rows), f32),
            pltpu.VMEM((4, slots, depth), bf16),
            pltpu.VMEM((4, slots, depth), bf16),
            pltpu.VMEM((4, slots, depth), bf16),
            pltpu.VMEM((NEAR, rows, depth), bf16),
            pltpu.VMEM((slots, width), bf16),
            pltpu.VMEM((2 * experts, 2 * rows), f32),
            pltpu.VMEM((experts, 2 * rows), f32),
            pltpu.VMEM((NEAR, experts, 2 * rows), f32),
            pltpu.VMEM((2, experts, 2 * rows), f32),
            dma((3,)),
            dma((NEAR,)), dma((NEAR,)),
            dma((NEAR,)), dma((NEAR,)),
            dma((4 * NEAR,)), dma((4 * NEAR,)),
            dma((4 * NEAR,)), dma((4 * NEAR,)),
            dma((NEAR,)), dma((NEAR,)),
            dma((NEAR,)), dma((NEAR,)),
            dma, dma,
        ],
        compiler_params=pltpu.CompilerParams(
            collective_id=0, has_side_effects=True, vmem_limit_bytes=60 * 1024 * 1024
        ),
    )(tokens, expert_ids, router_weight, gate_weight, up_weight, down_weight)
    return mixed, load[0, :experts]


def solution(mesh):
    return jax.shard_map(
        local,
        mesh=mesh,
        in_specs=(
            P(("dp", "expert"), None),
            P(("dp", "expert"), None),
            P(),
            P("expert", None, None),
            P("expert", None, None),
            P("expert", None, None),
        ),
        out_specs=(P(("dp", "expert"), None), P()),
        check_vma=False,
    )
```

```python
import functools

import jax
import jax.numpy as jnp
from jax import lax
from jax.experimental import pallas as pl
from jax.experimental.pallas import tpu as pltpu
from jax.sharding import PartitionSpec as P

MESH = pl.DeviceIdType.MESH
CAP = 16
NEAR = 8


def moe_kernel(
    sizes,
    tokens_ref, ids_ref, router_ref, wg_hbm, wu_hbm, wd_hbm,
    mixed_ref, load_ref,
    wg, wu, wd, gathered, routes, packed, served, back, sums, hidden, route, tally, tallies, twin,
    w_sem, g_send, g_recv, r_send, r_recv, d_send, d_recv, t_send, t_recv, p_send, p_recv,
    c_send, c_recv, x_send, x_recv,
):
    rows, depth, width, experts, top = sizes
    f32, bf16 = jnp.float32, jnp.bfloat16
    dp, me = lax.axis_index("dp"), lax.axis_index("expert")
    c = me % 2
    x = (me // 2) % 4
    y = (me // 8) % 4
    z = me // 32
    g = (1 - c) * y + c * x
    h = (1 - c) * x + c * y
    g_step, h_step = 8 - 6 * c, 2 + 6 * c
    my_place = h * 2 + c
    my_source = c * 4 + h
    slot_rows = 2 * CAP

    def offset_of(m):
        return m + (m // 2) * (1 - 2 * (m % 2))

    def chunk_there(m):
        return (m % 2) * 2 + m // 2

    def plane_device(m, q):
        return (z + q - 2 * z * q) * 32 + ((g + offset_of(m)) % 4) * g_step + h * h_step + c

    def served_device(place):
        return z * 32 + g * g_step + (place // 2) * h_step + place % 2

    def source_device(source):
        kind, far = source // 4, source % 4
        return z * 32 + (1 - kind) * (y * 8 + far * 2) + kind * (far * 8 + x * 2 + 1)

    def place_there(source):
        kind = source // 4
        return ((1 - kind) * x + kind * y) * 2 + c

    def rows_of(index):
        return pl.ds(pl.multiple_of(index * slot_rows, slot_rows), slot_rows)

    barrier = pltpu.get_barrier_semaphore()

    def greet(device):
        pl.semaphore_signal(barrier, inc=1, device_id=device, device_id_type=MESH)

    for i in range(1, NEAR):
        greet((dp, plane_device(i // 2, i % 2)))

    def greet_sets(k, carry):
        greet((dp, served_device((my_place + k) % NEAR)))
        greet((dp, source_device((my_source + k) % NEAR)))
        return carry

    lax.fori_loop(1, NEAR, greet_sets, 0)
    greet((1 - dp, me))

    weights = [
        pltpu.make_async_copy(wg_hbm.at[0], wg, w_sem.at[0]),
        pltpu.make_async_copy(wu_hbm.at[0], wu, w_sem.at[1]),
        pltpu.make_async_copy(wd_hbm.at[0], wd, w_sem.at[2]),
    ]
    for copy in weights:
        copy.start()

    gathered[0, 0:rows, :] = tokens_ref[...]
    pl.semaphore_wait(barrier, 3 * (NEAR - 1) + 1)

    def token_copy(i):
        m, q = i // 2, i % 2
        slot = chunk_there(m)
        relayed = m > 0 and q == 1
        return pltpu.make_async_remote_copy(
            src_ref=gathered.at[0, pl.ds(rows, rows)] if relayed else tokens_ref,
            dst_ref=gathered.at[slot, pl.ds(q * rows, rows)],
            send_sem=g_send.at[i],
            recv_sem=g_recv.at[slot * 2 + q],
            device_id=(dp, plane_device(m, 0 if relayed else q)),
            device_id_type=MESH,
        )

    def route_copy(i):
        m, q = i // 2, i % 2
        slot = chunk_there(m)
        return pltpu.make_async_remote_copy(
            src_ref=route,
            dst_ref=routes.at[slot, q],
            send_sem=r_send.at[i],
            recv_sem=r_recv.at[slot * 2 + q],
            device_id=(dp, plane_device(m, q)),
            device_id_type=MESH,
        )

    for i in (1, 2, 4):
        token_copy(i).start()

    logits = lax.dot_general(
        router_ref[...], tokens_ref[...], (((1,), (1,)), ((), ())), preferred_element_type=f32
    )
    expert_row = lax.broadcasted_iota(jnp.int32, (experts, rows), 0)
    chosen = jnp.zeros((experts, rows), f32)
    for k in range(top):
        chosen = jnp.where(ids_ref[k : k + 1, :] == expert_row, 1.0, chosen)
    affinity = jnp.where(chosen > 0, 1.0 / (1.0 + jnp.exp(-logits)), 0.0)
    gates = 2.5 * affinity / jnp.sum(affinity, axis=0, keepdims=True)
    earlier = lax.broadcasted_iota(jnp.int32, (rows, rows), 0)
    later = lax.broadcasted_iota(jnp.int32, (rows, rows), 1)
    upto = jnp.where(earlier <= later, 1.0, 0.0).astype(bf16)
    ranks = jnp.dot(chosen.astype(bf16), upto, preferred_element_type=f32)
    route[...] = jnp.concatenate([chosen * ranks, gates], axis=1)
    routes[0, 0] = route[...]
    for i in range(1, NEAR):
        route_copy(i).start()

    def landed(ref, sem):
        pltpu.make_async_copy(ref, ref, sem).wait()

    def wait_tokens(m, q):
        landed(gathered.at[m, pl.ds(q * rows, rows)], g_recv.at[m * 2 + q])

    def wait_route(m, q):
        landed(routes.at[m, q], r_recv.at[m * 2 + q])

    def spread(m, gate):
        half = lax.broadcasted_iota(jnp.int32, (NEAR, 2 * rows), 1) // rows

        def picked(q):
            table = [routes[m, q, pl.ds(served_device(place), 1), :] for place in range(NEAR)]
            table = jnp.concatenate(table, axis=0)
            return table if gate == q else jnp.concatenate([table[:, rows:], table[:, :rows]], axis=1)

        table = jnp.where(half == 0, picked(0), picked(1))
        table = jnp.broadcast_to(table[:, None, :], (NEAR, slot_rows, 2 * rows))
        return table.reshape(NEAR * slot_rows, 2 * rows)

    def taken(m):
        slot = lax.broadcasted_iota(jnp.int32, (NEAR * slot_rows, 2 * rows), 0) % slot_rows
        block = lax.broadcasted_iota(jnp.int32, (NEAR * slot_rows, 2 * rows), 1) // rows
        wanted = jnp.where(slot // CAP == block, slot % CAP + 1, -1).astype(f32)
        return spread(m, 0) == wanted

    def pack_chunk(m):
        select = jnp.where(taken(m), 1.0, 0.0).astype(bf16)

        def tile(n, carry):
            columns = pl.ds(pl.multiple_of(n * 512, 512), 512)
            packed[m, :, columns] = jnp.dot(
                select, gathered[m, :, columns], preferred_element_type=f32
            ).astype(bf16)
            return carry

        lax.fori_loop(0, depth // 512, tile, 0)

    def hand_out(m, k):
        place = (my_place + k) % NEAR
        return pltpu.make_async_remote_copy(
            src_ref=packed.at[m, rows_of(place)],
            dst_ref=served.at[m, rows_of(my_source)],
            send_sem=d_send.at[m * NEAR + k],
            recv_sem=d_recv.at[m * NEAR + my_source],
            device_id=(dp, served_device(place)),
            device_id_type=MESH,
        )

    def pack_and_send(m, carry):
        @pl.when(m > 0)
        def _():
            wait_tokens(m, 0)
            wait_route(m, 0)
            wait_tokens(m, 1)

        wait_route(m, 1)
        pack_chunk(m)

        def send(k, carry):
            hand_out(m, k).start()
            return carry

        lax.fori_loop(1, NEAR, send, 0)
        pltpu.make_async_copy(
            packed.at[m, rows_of(my_place)],
            served.at[m, rows_of(my_source)],
            d_recv.at[m * NEAR + my_source],
        ).start()
        return carry

    wait_tokens(0, 1)
    for i in (3, 5, 6, 7):
        token_copy(i).start()

    lax.fori_loop(0, 4, pack_and_send, 0)
    for i in range(1, NEAR):
        token_copy(i).wait_send()

    plane = jnp.zeros((experts, 2 * rows), f32)
    for i in range(NEAR):
        plane = plane + jnp.where(routes[i // 2, i % 2] > 0, 1.0, 0.0)
    ones = jnp.where(lax.broadcasted_iota(jnp.int32, (8, 2 * rows), 1) < rows, 1.0, 0.0).astype(bf16)
    tally[...] = jnp.zeros_like(tally)
    tally[:, 0:experts] = lax.dot_general(
        ones, plane.astype(bf16), (((1,), (1,)), ((), ())), preferred_element_type=f32
    )

    def tally_copy(k):
        return pltpu.make_async_remote_copy(
            src_ref=tally,
            dst_ref=tallies.at[my_source],
            send_sem=c_send.at[k],
            recv_sem=c_recv.at[my_source],
            device_id=(dp, served_device((my_place + k) % NEAR)),
            device_id_type=MESH,
        )

    def send_tally(k, carry):
        tally_copy(k).start()
        return carry

    lax.fori_loop(1, NEAR, send_tally, 0)
    pltpu.make_async_copy(tally, tallies.at[my_source], c_recv.at[my_source]).start()

    for copy in weights:
        copy.wait()

    def hand_back(m, k):
        source = (my_source + k) % NEAR
        place = place_there(source)
        return pltpu.make_async_remote_copy(
            src_ref=served.at[m, rows_of(source)],
            dst_ref=back.at[m, rows_of(place)],
            send_sem=t_send.at[m * NEAR + k],
            recv_sem=t_recv.at[m * NEAR + place],
            device_id=(dp, source_device(source)),
            device_id_type=MESH,
        )

    def serve(m, carry):
        def arrive(source, carry):
            landed(served.at[m, rows_of(source)], d_recv.at[m * NEAR + source])
            return carry

        lax.fori_loop(0, NEAR, arrive, 0)

        def into_hidden(n, carry):
            columns = pl.ds(pl.multiple_of(n * 256, 256), 256)
            gate_part = jnp.dot(served[m], wg[:, columns], preferred_element_type=f32)
            up_part = jnp.dot(served[m], wu[:, columns], preferred_element_type=f32)
            act = gate_part / (1.0 + jnp.exp(-gate_part)) * up_part
            hidden[:, columns] = act.astype(bf16)
            return carry

        lax.fori_loop(0, width // 256, into_hidden, 0)

        def out_of_hidden(n, carry):
            columns = pl.ds(pl.multiple_of(n * 512, 512), 512)
            served[m, :, columns] = jnp.dot(
                hidden[...], wd[:, columns], preferred_element_type=f32
            ).astype(bf16)
            return carry

        lax.fori_loop(0, depth // 512, out_of_hidden, 0)

        def send(k, carry):
            hand_back(m, k).start()
            return carry

        lax.fori_loop(1, NEAR, send, 0)
        pltpu.make_async_copy(
            served.at[m, rows_of(my_source)],
            back.at[m, rows_of(my_place)],
            t_recv.at[m * NEAR + my_place],
        ).start()
        return carry

    def sum_copy(m, q):
        slot = chunk_there(m)
        return pltpu.make_async_remote_copy(
            src_ref=gathered.at[m, pl.ds(q * rows, rows)],
            dst_ref=sums.at[slot * 2 + q],
            send_sem=p_send.at[m * 2 + q],
            recv_sem=p_recv.at[slot * 2 + q],
            device_id=(dp, plane_device(m, q)),
            device_id_type=MESH,
        )

    def combine(m, carry):
        def arrive(place, carry):
            landed(back.at[m, rows_of(place)], t_recv.at[m * NEAR + place])
            return carry

        lax.fori_loop(0, NEAR, arrive, 0)
        weight = jnp.where(taken(m), spread(m, 1), 0.0).T
        high = weight.astype(bf16)
        low = (weight - high.astype(f32)).astype(bf16)

        def tile(n, carry):
            columns = pl.ds(pl.multiple_of(n * 512, 512), 512)
            block = back[m, :, columns]
            total = jnp.dot(high, block, preferred_element_type=f32)
            total = total + jnp.dot(low, block, preferred_element_type=f32)
            gathered[m, :, columns] = total.astype(bf16)
            return carry

        lax.fori_loop(0, depth // 512, tile, 0)

        @pl.when(m > 0)
        def _():
            sum_copy(m, 0).start()

        sum_copy(m, 1).start()
        return carry

    def serve_and_combine(m, carry):
        serve(m, carry)

        @pl.when(m >= 2)
        def _():
            combine(m - 2, 0)

        return carry

    lax.fori_loop(0, 4, serve_and_combine, 0)

    group = jnp.zeros((8, 2 * experts), f32)
    for source in range(NEAR):
        landed(tallies.at[source], c_recv.at[source])
        group = group + tallies[source]
    twin[0] = group
    twin_copy = pltpu.make_async_remote_copy(
        src_ref=twin.at[0],
        dst_ref=twin.at[1],
        send_sem=x_send,
        recv_sem=x_recv,
        device_id=(1 - dp, me),
        device_id_type=MESH,
    )
    twin_copy.start()

    lax.fori_loop(2, 4, combine, 0)

    twin_copy.wait()
    load_ref[...] = (twin[0, 0:1, 0:experts] + twin[1, 0:1, 0:experts]) * (1.0 / 1024.0)

    for i in range(1, NEAR):
        route_copy(i).wait_send()

    def sent(k, carry):
        tally_copy(k).wait_send()

        def sent_chunk(m, carry):
            hand_out(m, k).wait_send()
            hand_back(m, k).wait_send()
            return carry

        return lax.fori_loop(0, 4, sent_chunk, carry)

    lax.fori_loop(1, NEAR, sent, 0)

    for i in range(1, NEAR):
        landed(sums.at[i], p_recv.at[i])

    def finish(n, carry):
        columns = pl.ds(pl.multiple_of(n * 512, 512), 512)
        total = gathered[0, 0:rows, columns].astype(f32)
        for i in range(1, NEAR):
            total = total + sums[i, :, columns].astype(f32)
        mixed_ref[:, columns] = total.astype(bf16)
        return carry

    lax.fori_loop(0, depth // 512, finish, 0)

    for i in range(1, NEAR):
        sum_copy(i // 2, i % 2).wait_send()


def local(tokens, expert_ids, router_weight, gate_weight, up_weight, down_weight):
    rows, depth = tokens.shape
    top = expert_ids.shape[1]
    experts = router_weight.shape[1]
    width = gate_weight.shape[2]
    bf16, f32 = jnp.bfloat16, jnp.float32
    slots = NEAR * 2 * CAP
    vmem = pl.BlockSpec(memory_space=pltpu.VMEM)
    hbm = pl.BlockSpec(memory_space=pl.ANY)
    dma = pltpu.SemaphoreType.DMA
    mixed, load = pl.pallas_call(
        functools.partial(moe_kernel, (rows, depth, width, experts, top)),
        out_shape=(
            jax.ShapeDtypeStruct((rows, depth), bf16),
            jax.ShapeDtypeStruct((1, experts), f32),
        ),
        in_specs=[vmem, vmem, vmem, hbm, hbm, hbm],
        out_specs=(vmem, vmem),
        scratch_shapes=[
            pltpu.VMEM((depth, width), bf16),
            pltpu.VMEM((depth, width), bf16),
            pltpu.VMEM((width, depth), bf16),
            pltpu.VMEM((4, 2 * rows, depth), bf16),
            pltpu.VMEM((4, 2, experts, 2 * rows), f32),
            pltpu.VMEM((4, slots, depth), bf16),
            pltpu.VMEM((4, slots, depth), bf16),
            pltpu.VMEM((4, slots, depth), bf16),
            pltpu.VMEM((NEAR, rows, depth), bf16),
            pltpu.VMEM((slots, width), bf16),
            pltpu.VMEM((experts, 2 * rows), f32),
            pltpu.VMEM((8, 2 * experts), f32),
            pltpu.VMEM((NEAR, 8, 2 * experts), f32),
            pltpu.VMEM((2, 8, 2 * experts), f32),
            dma((3,)),
            dma((NEAR,)), dma((NEAR,)),
            dma((NEAR,)), dma((NEAR,)),
            dma((4 * NEAR,)), dma((4 * NEAR,)),
            dma((4 * NEAR,)), dma((4 * NEAR,)),
            dma((NEAR,)), dma((NEAR,)),
            dma((NEAR,)), dma((NEAR,)),
            dma, dma,
        ],
        compiler_params=pltpu.CompilerParams(
            collective_id=0, has_side_effects=True, vmem_limit_bytes=60 * 1024 * 1024
        ),
    )(tokens, expert_ids.T, router_weight.T, gate_weight, up_weight, down_weight)
    return mixed, load.reshape(experts)


def solution(mesh):
    return jax.shard_map(
        local,
        mesh=mesh,
        in_specs=(
            P(("dp", "expert"), None),
            P(("dp", "expert"), None),
            P(),
            P("expert", None, None),
            P("expert", None, None),
            P("expert", None, None),
        ),
        out_specs=(P(("dp", "expert"), None), P()),
        check_vma=False,
    )
```

```python
import functools

import jax
import jax.numpy as jnp
from jax import lax
from jax.experimental import pallas as pl
from jax.experimental.pallas import tpu as pltpu
from jax.sharding import PartitionSpec as P

MESH = pl.DeviceIdType.MESH
VIA_PEER = (1, 2)
CAP = 16
NEAR = 8


def moe_kernel(
    sizes,
    tokens_ref, ids_ref, router_ref, wg_hbm, wu_hbm, wd_hbm,
    mixed_ref, load_ref,
    wg, wu, wd, gathered, routes, packed, served, back, sums, so_far, hidden, route, tally, tallies, twin,
    w_sem, g_send, g_recv, r_send, r_recv, d_send, d_recv, t_send, t_recv, p_send, p_recv,
    c_send, c_recv, x_send, x_recv,
):
    rows, depth, width, experts, top = sizes
    f32, bf16 = jnp.float32, jnp.bfloat16
    dp, me = lax.axis_index("dp"), lax.axis_index("expert")
    c = me % 2
    x = (me // 2) % 4
    y = (me // 8) % 4
    z = me // 32
    g = (1 - c) * y + c * x
    h = (1 - c) * x + c * y
    g_step, h_step = 8 - 6 * c, 2 + 6 * c
    my_place = h * 2 + c
    my_source = c * 4 + h
    slot_rows = 2 * CAP

    def offset_of(m):
        return m + (m // 2) * (1 - 2 * (m % 2))

    def chunk_there(m):
        return (m % 2) * 2 + m // 2

    def plane_device(m, q):
        return (z + q - 2 * z * q) * 32 + ((g + offset_of(m)) % 4) * g_step + h * h_step + c

    def served_device(place):
        return z * 32 + g * g_step + (place // 2) * h_step + place % 2

    def source_device(source):
        kind, far = source // 4, source % 4
        return z * 32 + (1 - kind) * (y * 8 + far * 2) + kind * (far * 8 + x * 2 + 1)

    def place_there(source):
        kind = source // 4
        return ((1 - kind) * x + kind * y) * 2 + c

    def rows_of(index):
        return pl.ds(pl.multiple_of(index * slot_rows, slot_rows), slot_rows)

    barrier = pltpu.get_barrier_semaphore()

    def greet(device):
        pl.semaphore_signal(barrier, inc=1, device_id=device, device_id_type=MESH)

    for i in range(1, NEAR):
        greet((dp, plane_device(i // 2, i % 2)))

    def greet_sets(k, carry):
        greet((dp, served_device((my_place + k) % NEAR)))
        greet((dp, source_device((my_source + k) % NEAR)))
        return carry

    lax.fori_loop(1, NEAR, greet_sets, 0)
    greet((1 - dp, me))

    weights = [
        pltpu.make_async_copy(wg_hbm.at[0], wg, w_sem.at[0]),
        pltpu.make_async_copy(wu_hbm.at[0], wu, w_sem.at[1]),
        pltpu.make_async_copy(wd_hbm.at[0], wd, w_sem.at[2]),
    ]
    for copy in weights:
        copy.start()

    gathered[0, 0:rows, :] = tokens_ref[...]
    pl.semaphore_wait(barrier, 3 * (NEAR - 1) + 1)

    def axis_copy(m):
        slot = chunk_there(m)
        return pltpu.make_async_remote_copy(
            src_ref=tokens_ref,
            dst_ref=gathered.at[slot, pl.ds(0, rows)],
            send_sem=g_send.at[m * 2],
            recv_sem=g_recv.at[slot * 2],
            device_id=(dp, plane_device(m, 0)),
            device_id_type=MESH,
        )

    def peer_copy(m):
        return pltpu.make_async_remote_copy(
            src_ref=gathered.at[m, pl.ds(0, rows)],
            dst_ref=gathered.at[m, pl.ds(rows, rows)],
            send_sem=g_send.at[m * 2 + 1],
            recv_sem=g_recv.at[m * 2 + 1],
            device_id=(dp, plane_device(0, 1)),
            device_id_type=MESH,
        )

    def route_copy(i):
        m, q = i // 2, i % 2
        slot = chunk_there(m)
        return pltpu.make_async_remote_copy(
            src_ref=route,
            dst_ref=routes.at[slot, q],
            send_sem=r_send.at[i],
            recv_sem=r_recv.at[slot * 2 + q],
            device_id=(dp, plane_device(m, q)),
            device_id_type=MESH,
        )

    peer_copy(0).start()
    for m in range(1, 4):
        axis_copy(m).start()

    logits = lax.dot_general(
        router_ref[...], tokens_ref[...], (((1,), (1,)), ((), ())), preferred_element_type=f32
    )
    expert_row = lax.broadcasted_iota(jnp.int32, (experts, rows), 0)
    chosen = jnp.zeros((experts, rows), f32)
    for k in range(top):
        chosen = jnp.where(ids_ref[k : k + 1, :] == expert_row, 1.0, chosen)
    affinity = jnp.where(chosen > 0, 1.0 / (1.0 + jnp.exp(-logits)), 0.0)
    gates = 2.5 * affinity / jnp.sum(affinity, axis=0, keepdims=True)
    earlier = lax.broadcasted_iota(jnp.int32, (rows, rows), 0)
    later = lax.broadcasted_iota(jnp.int32, (rows, rows), 1)
    upto = jnp.where(earlier <= later, 1.0, 0.0).astype(bf16)
    ranks = jnp.dot(chosen.astype(bf16), upto, preferred_element_type=f32)
    route[...] = jnp.concatenate([chosen * ranks, gates], axis=1)
    routes[0, 0] = route[...]
    for i in range(1, NEAR):
        route_copy(i).start()

    def landed(ref, sem):
        pltpu.make_async_copy(ref, ref, sem).wait()

    def wait_tokens(m, q):
        landed(gathered.at[m, pl.ds(q * rows, rows)], g_recv.at[m * 2 + q])

    def wait_route(m, q):
        landed(routes.at[m, q], r_recv.at[m * 2 + q])

    def spread(m, gate):
        half = lax.broadcasted_iota(jnp.int32, (NEAR, 2 * rows), 1) // rows

        def picked(q):
            table = [routes[m, q, pl.ds(served_device(place), 1), :] for place in range(NEAR)]
            table = jnp.concatenate(table, axis=0)
            return table if gate == q else jnp.concatenate([table[:, rows:], table[:, :rows]], axis=1)

        table = jnp.where(half == 0, picked(0), picked(1))
        table = jnp.broadcast_to(table[:, None, :], (NEAR, slot_rows, 2 * rows))
        return table.reshape(NEAR * slot_rows, 2 * rows)

    def taken(m):
        slot = lax.broadcasted_iota(jnp.int32, (NEAR * slot_rows, 2 * rows), 0) % slot_rows
        block = lax.broadcasted_iota(jnp.int32, (NEAR * slot_rows, 2 * rows), 1) // rows
        wanted = jnp.where(slot // CAP == block, slot % CAP + 1, -1).astype(f32)
        return spread(m, 0) == wanted

    def pack_chunk(m):
        select = jnp.where(taken(m), 1.0, 0.0).astype(bf16)

        def tile(n, carry):
            columns = pl.ds(pl.multiple_of(n * 512, 512), 512)
            packed[m, :, columns] = jnp.dot(
                select, gathered[m, :, columns], preferred_element_type=f32
            ).astype(bf16)
            return carry

        lax.fori_loop(0, depth // 512, tile, 0)

    def hand_out(m, k):
        place = (my_place + k) % NEAR
        return pltpu.make_async_remote_copy(
            src_ref=packed.at[m, rows_of(place)],
            dst_ref=served.at[m, rows_of(my_source)],
            send_sem=d_send.at[m * NEAR + k],
            recv_sem=d_recv.at[m * NEAR + my_source],
            device_id=(dp, served_device(place)),
            device_id_type=MESH,
        )

    def pack_and_send(m):
        wait_tokens(m, 1)

        @pl.when(m < 3)
        def _():
            wait_tokens(m + 1, 0)
            peer_copy(m + 1).start()

        @pl.when(m > 0)
        def _():
            wait_route(m, 0)

        wait_route(m, 1)
        pack_chunk(m)

        def send(k, carry):
            hand_out(m, k).start()
            return carry

        lax.fori_loop(1, NEAR, send, 0)
        pltpu.make_async_copy(
            packed.at[m, rows_of(my_place)],
            served.at[m, rows_of(my_source)],
            d_recv.at[m * NEAR + my_source],
        ).start()


    def hand_back(m, k):
        source = (my_source + k) % NEAR
        place = place_there(source)
        return pltpu.make_async_remote_copy(
            src_ref=served.at[m, rows_of(source)],
            dst_ref=back.at[m, rows_of(place)],
            send_sem=t_send.at[m * NEAR + k],
            recv_sem=t_recv.at[m * NEAR + place],
            device_id=(dp, source_device(source)),
            device_id_type=MESH,
        )

    def serve(m, carry):
        def arrive(source, carry):
            landed(served.at[m, rows_of(source)], d_recv.at[m * NEAR + source])
            return carry

        lax.fori_loop(0, NEAR, arrive, 0)

        def into_hidden(n, carry):
            columns = pl.ds(pl.multiple_of(n * 256, 256), 256)
            gate_part = jnp.dot(served[m], wg[:, columns], preferred_element_type=f32)
            up_part = jnp.dot(served[m], wu[:, columns], preferred_element_type=f32)
            act = gate_part / (1.0 + jnp.exp(-gate_part)) * up_part
            hidden[:, columns] = act.astype(bf16)
            return carry

        lax.fori_loop(0, width // 256, into_hidden, 0)

        def out_of_hidden(n, carry):
            columns = pl.ds(pl.multiple_of(n * 512, 512), 512)
            served[m, :, columns] = jnp.dot(
                hidden[...], wd[:, columns], preferred_element_type=f32
            ).astype(bf16)
            return carry

        lax.fori_loop(0, depth // 512, out_of_hidden, 0)

        def send(k, carry):
            hand_back(m, k).start()
            return carry

        lax.fori_loop(1, NEAR, send, 0)
        pltpu.make_async_copy(
            served.at[m, rows_of(my_source)],
            back.at[m, rows_of(my_place)],
            t_recv.at[m * NEAR + my_place],
        ).start()
        return carry

    def sum_copy(m, q):
        slot = chunk_there(m)
        return pltpu.make_async_remote_copy(
            src_ref=gathered.at[m, pl.ds(q * rows, rows)],
            dst_ref=sums.at[slot * 2 + q],
            send_sem=p_send.at[m * 2 + q],
            recv_sem=p_recv.at[slot * 2 + q],
            device_id=(dp, plane_device(m, q)),
            device_id_type=MESH,
        )

    def peer_sum_copy(m):
        return pltpu.make_async_remote_copy(
            src_ref=gathered.at[m, pl.ds(rows, rows)],
            dst_ref=sums.at[m * 2 + 1],
            send_sem=p_send.at[m * 2 + 1],
            recv_sem=p_recv.at[m * 2 + 1],
            device_id=(dp, plane_device(0, 1)),
            device_id_type=MESH,
        )

    def combine(m):
        peer_copy(m).wait_send()
        def arrive(place, carry):
            landed(back.at[m, rows_of(place)], t_recv.at[m * NEAR + place])
            return carry

        lax.fori_loop(0, NEAR, arrive, 0)
        weight = jnp.where(taken(m), spread(m, 1), 0.0).T
        high = weight.astype(bf16)
        low = (weight - high.astype(f32)).astype(bf16)

        def tile(n, carry):
            columns = pl.ds(pl.multiple_of(n * 512, 512), 512)
            block = back[m, :, columns]
            total = jnp.dot(high, block, preferred_element_type=f32)
            total = total + jnp.dot(low, block, preferred_element_type=f32)
            gathered[m, :, columns] = total.astype(bf16)
            return carry

        lax.fori_loop(0, depth // 512, tile, 0)

        if m in VIA_PEER:
            peer_sum_copy(m).start()
        else:
            if m > 0:
                sum_copy(m, 0).start()
            sum_copy(m, 1).start()

    def pass_on(m):
        landed(sums.at[m * 2 + 1], p_recv.at[m * 2 + 1])

        def tile(n, carry):
            columns = pl.ds(pl.multiple_of(n * 512, 512), 512)
            both = gathered[m, 0:rows, columns].astype(f32) + sums[m * 2 + 1, :, columns].astype(f32)
            gathered[m, 0:rows, columns] = both.astype(bf16)
            return carry

        lax.fori_loop(0, depth // 512, tile, 0)
        sum_copy(m, 0).start()

    def pack_first(m, carry):
        pack_and_send(m)
        return carry

    lax.fori_loop(0, 2, pack_first, 0)
    for copy in weights:
        copy.wait()

    def serve_and_pack(m, carry):
        serve(m, carry)
        pack_and_send(m + 2)
        return carry

    lax.fori_loop(0, 2, serve_and_pack, 0)
    combine(0)
    serve(2, 0)
    combine(1)
    serve(3, 0)
    pass_on(1)
    combine(2)

    plane = jnp.zeros((experts, 2 * rows), f32)
    for i in range(NEAR):
        plane = plane + jnp.where(routes[i // 2, i % 2] > 0, 1.0, 0.0)
    ones = jnp.where(lax.broadcasted_iota(jnp.int32, (8, 2 * rows), 1) < rows, 1.0, 0.0).astype(bf16)
    tally[...] = jnp.zeros_like(tally)
    tally[:, 0:experts] = lax.dot_general(
        ones, plane.astype(bf16), (((1,), (1,)), ((), ())), preferred_element_type=f32
    )

    def tally_copy(k):
        return pltpu.make_async_remote_copy(
            src_ref=tally,
            dst_ref=tallies.at[my_source],
            send_sem=c_send.at[k],
            recv_sem=c_recv.at[my_source],
            device_id=(dp, served_device((my_place + k) % NEAR)),
            device_id_type=MESH,
        )

    def send_tally(k, carry):
        tally_copy(k).start()
        return carry

    lax.fori_loop(1, NEAR, send_tally, 0)
    pltpu.make_async_copy(tally, tallies.at[my_source], c_recv.at[my_source]).start()


    group = jnp.zeros((8, 2 * experts), f32)
    for source in range(NEAR):
        landed(tallies.at[source], c_recv.at[source])
        group = group + tallies[source]
    twin[0] = group
    twin_copy = pltpu.make_async_remote_copy(
        src_ref=twin.at[0],
        dst_ref=twin.at[1],
        send_sem=x_send,
        recv_sem=x_recv,
        device_id=(1 - dp, me),
        device_id_type=MESH,
    )
    twin_copy.start()

    pass_on(2)
    combine(3)
    if 3 in VIA_PEER:
        pass_on(3)

    twin_copy.wait()
    load_ref[...] = (twin[0, 0:1, 0:experts] + twin[1, 0:1, 0:experts]) * (1.0 / 1024.0)

    for m in range(1, 4):
        axis_copy(m).wait_send()
    for i in range(1, NEAR):
        route_copy(i).wait_send()

    def sent(k, carry):
        tally_copy(k).wait_send()

        def sent_chunk(m, carry):
            hand_out(m, k).wait_send()
            hand_back(m, k).wait_send()
            return carry

        return lax.fori_loop(0, 4, sent_chunk, carry)

    lax.fori_loop(1, NEAR, sent, 0)

    early, late = [1, 2, 4], [6] if 3 in VIA_PEER else [6, 7]
    for i in early:
        landed(sums.at[i], p_recv.at[i])

    def gather_early(n, carry):
        columns = pl.ds(pl.multiple_of(n * 512, 512), 512)
        total = gathered[0, 0:rows, columns].astype(f32)
        for i in early:
            total = total + sums[i, :, columns].astype(f32)
        so_far[:, columns] = total
        return carry

    lax.fori_loop(0, depth // 512, gather_early, 0)
    for i in late:
        landed(sums.at[i], p_recv.at[i])

    def finish(n, carry):
        columns = pl.ds(pl.multiple_of(n * 512, 512), 512)
        total = so_far[:, columns]
        for i in late:
            total = total + sums[i, :, columns].astype(f32)
        mixed_ref[:, columns] = total.astype(bf16)
        return carry

    lax.fori_loop(0, depth // 512, finish, 0)
    sum_copy(0, 1).wait_send()
    for m in range(1, 4):
        sum_copy(m, 0).wait_send()
        (peer_sum_copy(m) if m in VIA_PEER else sum_copy(m, 1)).wait_send()


def local(tokens, expert_ids, router_weight, gate_weight, up_weight, down_weight):
    rows, depth = tokens.shape
    top = expert_ids.shape[1]
    experts = router_weight.shape[1]
    width = gate_weight.shape[2]
    bf16, f32 = jnp.bfloat16, jnp.float32
    slots = NEAR * 2 * CAP
    vmem = pl.BlockSpec(memory_space=pltpu.VMEM)
    hbm = pl.BlockSpec(memory_space=pl.ANY)
    dma = pltpu.SemaphoreType.DMA
    mixed, load = pl.pallas_call(
        functools.partial(moe_kernel, (rows, depth, width, experts, top)),
        out_shape=(
            jax.ShapeDtypeStruct((rows, depth), bf16),
            jax.ShapeDtypeStruct((1, experts), f32),
        ),
        in_specs=[vmem, vmem, vmem, hbm, hbm, hbm],
        out_specs=(vmem, vmem),
        scratch_shapes=[
            pltpu.VMEM((depth, width), bf16),
            pltpu.VMEM((depth, width), bf16),
            pltpu.VMEM((width, depth), bf16),
            pltpu.VMEM((4, 2 * rows, depth), bf16),
            pltpu.VMEM((4, 2, experts, 2 * rows), f32),
            pltpu.VMEM((4, slots, depth), bf16),
            pltpu.VMEM((4, slots, depth), bf16),
            pltpu.VMEM((4, slots, depth), bf16),
            pltpu.VMEM((NEAR, rows, depth), bf16),
            pltpu.VMEM((rows, depth), f32),
            pltpu.VMEM((slots, width), bf16),
            pltpu.VMEM((experts, 2 * rows), f32),
            pltpu.VMEM((8, 2 * experts), f32),
            pltpu.VMEM((NEAR, 8, 2 * experts), f32),
            pltpu.VMEM((2, 8, 2 * experts), f32),
            dma((3,)),
            dma((NEAR,)), dma((NEAR,)),
            dma((NEAR,)), dma((NEAR,)),
            dma((4 * NEAR,)), dma((4 * NEAR,)),
            dma((4 * NEAR,)), dma((4 * NEAR,)),
            dma((NEAR,)), dma((NEAR,)),
            dma((NEAR,)), dma((NEAR,)),
            dma, dma,
        ],
        compiler_params=pltpu.CompilerParams(
            collective_id=0, has_side_effects=True, vmem_limit_bytes=60 * 1024 * 1024
        ),
    )(tokens, expert_ids.T, router_weight.T, gate_weight, up_weight, down_weight)
    return mixed, load.reshape(experts)


def solution(mesh):
    return jax.shard_map(
        local,
        mesh=mesh,
        in_specs=(
            P(("dp", "expert"), None),
            P(("dp", "expert"), None),
            P(),
            P("expert", None, None),
            P("expert", None, None),
            P("expert", None, None),
        ),
        out_specs=(P(("dp", "expert"), None), P()),
        check_vma=False,
    )
```

```python
import functools

import jax
import jax.numpy as jnp
from jax import lax
from jax.experimental import pallas as pl
from jax.experimental.pallas import tpu as pltpu
from jax.sharding import PartitionSpec as P

MESH = pl.DeviceIdType.MESH
CHUNKS = (((1, 0), (2, 0)), ((0, 1), (1, 1)), ((3, 0), (2, 1)), ((0, 0), (3, 1)))
VIA_PEER = (1, 2)
FORWARD = {(1, 0): 1, (0, 1): 2, (1, 1): 3}
CAP = 16
NEAR = 8


def moe_kernel(
    sizes,
    tokens_ref, ids_ref, router_ref, wg_hbm, wu_hbm, wd_hbm,
    mixed_ref, load_ref,
    wg, wu, wd, gathered, routes, packed, served, back, sums, so_far, hidden, route, tally, tallies, twin,
    w_sem, g_send, g_recv, r_send, r_recv, d_send, d_recv, t_send, t_recv, p_send, p_recv,
    c_send, c_recv, x_send, x_recv,
):
    rows, depth, width, experts, top = sizes
    f32, bf16 = jnp.float32, jnp.bfloat16
    dp, me = lax.axis_index("dp"), lax.axis_index("expert")
    c = me % 2
    x = (me // 2) % 4
    y = (me // 8) % 4
    z = me // 32
    g = (1 - c) * y + c * x
    h = (1 - c) * x + c * y
    g_step, h_step = 8 - 6 * c, 2 + 6 * c
    my_place = h * 2 + c
    my_source = c * 4 + h
    slot_rows = 2 * CAP

    def offset_of(m):
        return m + (m // 2) * (1 - 2 * (m % 2))

    def chunk_there(m):
        return (m % 2) * 2 + m // 2

    def plane_device(m, q):
        return (z + q - 2 * z * q) * 32 + ((g + offset_of(m)) % 4) * g_step + h * h_step + c

    def served_device(place):
        return z * 32 + g * g_step + (place // 2) * h_step + place % 2

    def source_device(source):
        kind, far = source // 4, source % 4
        return z * 32 + (1 - kind) * (y * 8 + far * 2) + kind * (far * 8 + x * 2 + 1)

    def place_there(source):
        kind = source // 4
        return ((1 - kind) * x + kind * y) * 2 + c

    def rows_of(index):
        return pl.ds(pl.multiple_of(index * slot_rows, slot_rows), slot_rows)

    barrier = pltpu.get_barrier_semaphore()

    def greet(device):
        pl.semaphore_signal(barrier, inc=1, device_id=device, device_id_type=MESH)

    for i in range(1, NEAR):
        greet((dp, plane_device(i // 2, i % 2)))

    def greet_sets(k, carry):
        greet((dp, served_device((my_place + k) % NEAR)))
        greet((dp, source_device((my_source + k) % NEAR)))
        return carry

    lax.fori_loop(1, NEAR, greet_sets, 0)
    greet((1 - dp, me))

    weights = [
        pltpu.make_async_copy(wg_hbm.at[0], wg, w_sem.at[0]),
        pltpu.make_async_copy(wu_hbm.at[0], wu, w_sem.at[1]),
        pltpu.make_async_copy(wd_hbm.at[0], wd, w_sem.at[2]),
    ]
    for copy in weights:
        copy.start()

    gathered[0, 0:rows, :] = tokens_ref[...]
    pl.semaphore_wait(barrier, 3 * (NEAR - 1) + 1)

    def axis_copy(m):
        slot = chunk_there(m)
        return pltpu.make_async_remote_copy(
            src_ref=tokens_ref,
            dst_ref=gathered.at[slot, pl.ds(0, rows)],
            send_sem=g_send.at[m * 2],
            recv_sem=g_recv.at[slot * 2],
            device_id=(dp, plane_device(m, 0)),
            device_id_type=MESH,
        )

    def peer_copy(m):
        return pltpu.make_async_remote_copy(
            src_ref=gathered.at[m, pl.ds(0, rows)],
            dst_ref=gathered.at[m, pl.ds(rows, rows)],
            send_sem=g_send.at[m * 2 + 1],
            recv_sem=g_recv.at[m * 2 + 1],
            device_id=(dp, plane_device(0, 1)),
            device_id_type=MESH,
        )

    def route_copy(i):
        m, q = i // 2, i % 2
        slot = chunk_there(m)
        return pltpu.make_async_remote_copy(
            src_ref=route,
            dst_ref=routes.at[slot, q],
            send_sem=r_send.at[i],
            recv_sem=r_recv.at[slot * 2 + q],
            device_id=(dp, plane_device(m, q)),
            device_id_type=MESH,
        )

    peer_copy(0).start()
    for m in range(1, 4):
        axis_copy(m).start()

    logits = lax.dot_general(
        router_ref[...], tokens_ref[...], (((1,), (1,)), ((), ())), preferred_element_type=f32
    )
    expert_row = lax.broadcasted_iota(jnp.int32, (experts, rows), 0)
    chosen = jnp.zeros((experts, rows), f32)
    for k in range(top):
        chosen = jnp.where(ids_ref[k : k + 1, :] == expert_row, 1.0, chosen)
    affinity = jnp.where(chosen > 0, 1.0 / (1.0 + jnp.exp(-logits)), 0.0)
    gates = 2.5 * affinity / jnp.sum(affinity, axis=0, keepdims=True)
    earlier = lax.broadcasted_iota(jnp.int32, (rows, rows), 0)
    later = lax.broadcasted_iota(jnp.int32, (rows, rows), 1)
    upto = jnp.where(earlier <= later, 1.0, 0.0).astype(bf16)
    ranks = jnp.dot(chosen.astype(bf16), upto, preferred_element_type=f32)
    route[...] = jnp.concatenate([chosen * ranks, gates], axis=1)
    routes[0, 0] = route[...]
    for i in range(1, NEAR):
        route_copy(i).start()

    def landed(ref, sem):
        pltpu.make_async_copy(ref, ref, sem).wait()

    def wait_tokens(m, q):
        landed(gathered.at[m, pl.ds(q * rows, rows)], g_recv.at[m * 2 + q])

    def wait_route(m, q):
        landed(routes.at[m, q], r_recv.at[m * 2 + q])

    def table(m, q):
        picked = [routes[m, q, pl.ds(served_device(place), 1), :] for place in range(NEAR)]
        return jnp.concatenate(picked, axis=0)

    def per_slot(values, count):
        values = jnp.broadcast_to(values[:, None, :], (NEAR, count, values.shape[1]))
        return values.reshape(NEAR * count, values.shape[2])

    def pack_block(j, w):
        m, q = CHUNKS[j][w]
        codes = per_slot(table(m, q)[:, :rows], CAP)
        slot = lax.broadcasted_iota(jnp.int32, (NEAR * CAP, rows), 0) % CAP
        select = jnp.where(codes == (slot + 1).astype(f32), 1.0, 0.0).astype(bf16)

        def tile(n, carry):
            columns = pl.ds(pl.multiple_of(n * 512, 512), 512)
            block = gathered[m, q * rows : (q + 1) * rows, columns]
            packed[j, w, :, columns] = jnp.dot(select, block, preferred_element_type=f32).astype(bf16)
            return carry

        lax.fori_loop(0, depth // 512, tile, 0)

    def weights_of(j):
        (m, q), (far_m, far_q) = CHUNKS[j]
        near, far = table(m, q), table(far_m, far_q)
        half = lax.broadcasted_iota(jnp.int32, (NEAR, 2 * rows), 1) < rows
        swap = lambda t: jnp.concatenate([t[:, rows:], t[:, :rows]], axis=1)
        codes = per_slot(jnp.where(half, near, swap(far)), slot_rows)
        gates = per_slot(jnp.where(half, swap(near), far), slot_rows)
        slot = lax.broadcasted_iota(jnp.int32, (NEAR * slot_rows, 2 * rows), 0) % slot_rows
        block = lax.broadcasted_iota(jnp.int32, (NEAR * slot_rows, 2 * rows), 1) // rows
        wanted = jnp.where(slot // CAP == block, slot % CAP + 1, -1).astype(f32)
        return jnp.where(codes == wanted, gates, 0.0)

    def hand_out(i, k):
        place = (my_place + k) % NEAR
        j, w = i // 2, i % 2
        return pltpu.make_async_remote_copy(
            src_ref=packed.at[j, w, pl.ds(pl.multiple_of(place * CAP, CAP), CAP)],
            dst_ref=served.at[j, half_rows_of(my_source, w)],
            send_sem=d_send.at[i * NEAR + k],
            recv_sem=d_recv.at[i * NEAR + my_source],
            device_id=(dp, served_device(place)),
            device_id_type=MESH,
        )

    def half_rows_of(index, w):
        return pl.ds(pl.multiple_of(index * slot_rows + w * CAP, CAP), CAP)

    def pack_and_send(j, w):
        m, q = CHUNKS[j][w]
        if (m, q) != (0, 0):
            wait_tokens(m, q)
            wait_route(m, q)
        if (m, q) in FORWARD:
            peer_copy(FORWARD[m, q]).start()
        pack_block(j, w)
        i = j * 2 + w

        def send(k, carry):
            hand_out(i, k).start()
            return carry

        lax.fori_loop(1, NEAR, send, 0)
        pltpu.make_async_copy(
            packed.at[j, w, pl.ds(pl.multiple_of(my_place * CAP, CAP), CAP)],
            served.at[j, half_rows_of(my_source, w)],
            d_recv.at[i * NEAR + my_source],
        ).start()

    def hand_back(m, k):
        source = (my_source + k) % NEAR
        place = place_there(source)
        return pltpu.make_async_remote_copy(
            src_ref=served.at[m, rows_of(source)],
            dst_ref=back.at[m, rows_of(place)],
            send_sem=t_send.at[m * NEAR + k],
            recv_sem=t_recv.at[m * NEAR + place],
            device_id=(dp, source_device(source)),
            device_id_type=MESH,
        )

    def serve(m, carry):
        def arrive(source, carry):
            landed(served.at[m, half_rows_of(source, 0)], d_recv.at[m * 2 * NEAR + source])
            landed(served.at[m, half_rows_of(source, 1)], d_recv.at[(m * 2 + 1) * NEAR + source])
            return carry

        lax.fori_loop(0, NEAR, arrive, 0)

        def into_hidden(n, carry):
            columns = pl.ds(pl.multiple_of(n * 256, 256), 256)
            gate_part = jnp.dot(served[m], wg[:, columns], preferred_element_type=f32)
            up_part = jnp.dot(served[m], wu[:, columns], preferred_element_type=f32)
            act = gate_part / (1.0 + jnp.exp(-gate_part)) * up_part
            hidden[:, columns] = act.astype(bf16)
            return carry

        lax.fori_loop(0, width // 256, into_hidden, 0)

        def out_of_hidden(n, carry):
            columns = pl.ds(pl.multiple_of(n * 512, 512), 512)
            served[m, :, columns] = jnp.dot(
                hidden[...], wd[:, columns], preferred_element_type=f32
            ).astype(bf16)
            return carry

        lax.fori_loop(0, depth // 512, out_of_hidden, 0)

        def send(k, carry):
            hand_back(m, k).start()
            return carry

        lax.fori_loop(1, NEAR, send, 0)
        pltpu.make_async_copy(
            served.at[m, rows_of(my_source)],
            back.at[m, rows_of(my_place)],
            t_recv.at[m * NEAR + my_place],
        ).start()
        return carry

    def sum_copy(m, q):
        slot = chunk_there(m)
        return pltpu.make_async_remote_copy(
            src_ref=gathered.at[m, pl.ds(q * rows, rows)],
            dst_ref=sums.at[slot * 2 + q],
            send_sem=p_send.at[m * 2 + q],
            recv_sem=p_recv.at[slot * 2 + q],
            device_id=(dp, plane_device(m, q)),
            device_id_type=MESH,
        )

    def peer_sum_copy(m):
        return pltpu.make_async_remote_copy(
            src_ref=gathered.at[m, pl.ds(rows, rows)],
            dst_ref=sums.at[m * 2 + 1],
            send_sem=p_send.at[m * 2 + 1],
            recv_sem=p_recv.at[m * 2 + 1],
            device_id=(dp, plane_device(0, 1)),
            device_id_type=MESH,
        )

    def combine(j):
        (m, q), (far_m, far_q) = CHUNKS[j]

        def arrive(place, carry):
            landed(back.at[j, rows_of(place)], t_recv.at[j * NEAR + place])
            return carry

        lax.fori_loop(0, NEAR, arrive, 0)
        for place, other in CHUNKS[j]:
            if other == 0:
                peer_copy(place).wait_send()
        weight = weights_of(j).T
        high = weight.astype(bf16)
        low = (weight - high.astype(f32)).astype(bf16)

        def tile(n, carry):
            columns = pl.ds(pl.multiple_of(n * 512, 512), 512)
            block = back[j, :, columns]
            total = jnp.dot(high, block, preferred_element_type=f32)
            total = (total + jnp.dot(low, block, preferred_element_type=f32)).astype(bf16)
            gathered[m, q * rows : (q + 1) * rows, columns] = total[:rows]
            gathered[far_m, far_q * rows : (far_q + 1) * rows, columns] = total[rows:]
            return carry

        lax.fori_loop(0, depth // 512, tile, 0)
        for place, other in CHUNKS[j]:
            if place in VIA_PEER:
                if other == 1:
                    peer_sum_copy(place).start()
            elif (place, other) != (0, 0):
                sum_copy(place, other).start()

    def pass_on(m):
        landed(sums.at[m * 2 + 1], p_recv.at[m * 2 + 1])

        def tile(n, carry):
            columns = pl.ds(pl.multiple_of(n * 512, 512), 512)
            both = gathered[m, 0:rows, columns].astype(f32) + sums[m * 2 + 1, :, columns].astype(f32)
            gathered[m, 0:rows, columns] = both.astype(bf16)
            return carry

        lax.fori_loop(0, depth // 512, tile, 0)
        sum_copy(m, 0).start()

    def serve_chunk(m):
        lax.fori_loop(m, m + 1, serve, 0)

    for j, w in ((3, 0), (0, 0), (0, 1), (2, 0), (1, 0), (1, 1)):
        pack_and_send(j, w)
    for copy in weights:
        copy.wait()
    serve_chunk(0)
    pack_and_send(2, 1)
    serve_chunk(1)
    pack_and_send(3, 1)
    combine(0)
    serve_chunk(2)
    combine(1)
    serve_chunk(3)
    combine(2)
    pass_on(1)

    plane = jnp.zeros((experts, 2 * rows), f32)
    for i in range(NEAR):
        plane = plane + jnp.where(routes[i // 2, i % 2] > 0, 1.0, 0.0)
    ones = jnp.where(lax.broadcasted_iota(jnp.int32, (8, 2 * rows), 1) < rows, 1.0, 0.0).astype(bf16)
    tally[...] = jnp.zeros_like(tally)
    tally[:, 0:experts] = lax.dot_general(
        ones, plane.astype(bf16), (((1,), (1,)), ((), ())), preferred_element_type=f32
    )

    def tally_copy(k):
        return pltpu.make_async_remote_copy(
            src_ref=tally,
            dst_ref=tallies.at[my_source],
            send_sem=c_send.at[k],
            recv_sem=c_recv.at[my_source],
            device_id=(dp, served_device((my_place + k) % NEAR)),
            device_id_type=MESH,
        )

    def send_tally(k, carry):
        tally_copy(k).start()
        return carry

    lax.fori_loop(1, NEAR, send_tally, 0)
    pltpu.make_async_copy(tally, tallies.at[my_source], c_recv.at[my_source]).start()


    group = jnp.zeros((8, 2 * experts), f32)
    for source in range(NEAR):
        landed(tallies.at[source], c_recv.at[source])
        group = group + tallies[source]
    twin[0] = group
    twin_copy = pltpu.make_async_remote_copy(
        src_ref=twin.at[0],
        dst_ref=twin.at[1],
        send_sem=x_send,
        recv_sem=x_recv,
        device_id=(1 - dp, me),
        device_id_type=MESH,
    )
    twin_copy.start()

    combine(3)
    pass_on(2)

    twin_copy.wait()
    load_ref[...] = (twin[0, 0:1, 0:experts] + twin[1, 0:1, 0:experts]) * (1.0 / 1024.0)

    for m in range(1, 4):
        axis_copy(m).wait_send()
    for i in range(1, NEAR):
        route_copy(i).wait_send()

    def sent(k, carry):
        tally_copy(k).wait_send()

        def sent_chunk(m, carry):
            hand_out(m * 2, k).wait_send()
            hand_out(m * 2 + 1, k).wait_send()
            hand_back(m, k).wait_send()
            return carry

        return lax.fori_loop(0, 4, sent_chunk, carry)

    lax.fori_loop(1, NEAR, sent, 0)

    early, late = [1, 4, 6], [2, 7]
    for i in early:
        landed(sums.at[i], p_recv.at[i])

    def gather_early(n, carry):
        columns = pl.ds(pl.multiple_of(n * 512, 512), 512)
        total = gathered[0, 0:rows, columns].astype(f32)
        for i in early:
            total = total + sums[i, :, columns].astype(f32)
        so_far[:, columns] = total
        return carry

    lax.fori_loop(0, depth // 512, gather_early, 0)
    for i in late:
        landed(sums.at[i], p_recv.at[i])

    def finish(n, carry):
        columns = pl.ds(pl.multiple_of(n * 512, 512), 512)
        total = so_far[:, columns]
        for i in late:
            total = total + sums[i, :, columns].astype(f32)
        mixed_ref[:, columns] = total.astype(bf16)
        return carry

    lax.fori_loop(0, depth // 512, finish, 0)
    sum_copy(0, 1).wait_send()
    for m in range(1, 4):
        sum_copy(m, 0).wait_send()
        (peer_sum_copy(m) if m in VIA_PEER else sum_copy(m, 1)).wait_send()


def local(tokens, expert_ids, router_weight, gate_weight, up_weight, down_weight):
    rows, depth = tokens.shape
    top = expert_ids.shape[1]
    experts = router_weight.shape[1]
    width = gate_weight.shape[2]
    bf16, f32 = jnp.bfloat16, jnp.float32
    slots = NEAR * 2 * CAP
    vmem = pl.BlockSpec(memory_space=pltpu.VMEM)
    hbm = pl.BlockSpec(memory_space=pl.ANY)
    dma = pltpu.SemaphoreType.DMA
    mixed, load = pl.pallas_call(
        functools.partial(moe_kernel, (rows, depth, width, experts, top)),
        out_shape=(
            jax.ShapeDtypeStruct((rows, depth), bf16),
            jax.ShapeDtypeStruct((1, experts), f32),
        ),
        in_specs=[vmem, vmem, vmem, hbm, hbm, hbm],
        out_specs=(vmem, vmem),
        scratch_shapes=[
            pltpu.VMEM((depth, width), bf16),
            pltpu.VMEM((depth, width), bf16),
            pltpu.VMEM((width, depth), bf16),
            pltpu.VMEM((4, 2 * rows, depth), bf16),
            pltpu.VMEM((4, 2, experts, 2 * rows), f32),
            pltpu.VMEM((4, 2, NEAR * CAP, depth), bf16),
            pltpu.VMEM((4, slots, depth), bf16),
            pltpu.VMEM((4, slots, depth), bf16),
            pltpu.VMEM((NEAR, rows, depth), bf16),
            pltpu.VMEM((rows, depth), f32),
            pltpu.VMEM((slots, width), bf16),
            pltpu.VMEM((experts, 2 * rows), f32),
            pltpu.VMEM((8, 2 * experts), f32),
            pltpu.VMEM((NEAR, 8, 2 * experts), f32),
            pltpu.VMEM((2, 8, 2 * experts), f32),
            dma((3,)),
            dma((NEAR,)), dma((NEAR,)),
            dma((NEAR,)), dma((NEAR,)),
            dma((8 * NEAR,)), dma((8 * NEAR,)),
            dma((4 * NEAR,)), dma((4 * NEAR,)),
            dma((NEAR,)), dma((NEAR,)),
            dma((NEAR,)), dma((NEAR,)),
            dma, dma,
        ],
        compiler_params=pltpu.CompilerParams(
            collective_id=0, has_side_effects=True, vmem_limit_bytes=60 * 1024 * 1024
        ),
    )(tokens, expert_ids.T, router_weight.T, gate_weight, up_weight, down_weight)
    return mixed, load.reshape(experts)


def solution(mesh):
    return jax.shard_map(
        local,
        mesh=mesh,
        in_specs=(
            P(("dp", "expert"), None),
            P(("dp", "expert"), None),
            P(),
            P("expert", None, None),
            P("expert", None, None),
            P("expert", None, None),
        ),
        out_specs=(P(("dp", "expert"), None), P()),
        check_vma=False,
    )
```

```python
import functools

import jax
import jax.numpy as jnp
from jax import lax
from jax.experimental import pallas as pl
from jax.experimental.pallas import tpu as pltpu
from jax.sharding import PartitionSpec as P

MESH = pl.DeviceIdType.MESH
CHUNKS = (((1, 0), (2, 0)), ((0, 1), (1, 1)), ((3, 0), (2, 1)), ((0, 0), (3, 1)))
VIA_PEER = (1, 2)
FORWARD = {(1, 0): 1, (0, 1): 2, (1, 1): 3}
PARTS = ((0, 4), (4, 7))
CAP = 16
NEAR = 8


def moe_kernel(
    sizes,
    tokens_ref, ids_ref, router_ref, wg_hbm, wu_hbm, wd_hbm,
    mixed_ref, load_ref,
    wg, wu, wd, gathered, routes, packed, served, back, sums, so_far, hidden, route, tally, tallies, twin,
    w_sem, g_send, g_recv, r_send, r_recv, d_send, d_recv, t_send, t_recv, p_send, p_recv,
    c_send, c_recv, x_send, x_recv, l_send, l_recv,
):
    rows, depth, width, experts, top = sizes
    f32, bf16 = jnp.float32, jnp.bfloat16
    dp, me = lax.axis_index("dp"), lax.axis_index("expert")
    c = me % 2
    x = (me // 2) % 4
    y = (me // 8) % 4
    z = me // 32
    g = (1 - c) * y + c * x
    h = (1 - c) * x + c * y
    g_step, h_step = 8 - 6 * c, 2 + 6 * c
    my_place = h * 2 + c
    my_source = c * 4 + h
    slot_rows = 2 * CAP

    def offset_of(m):
        return m + (m // 2) * (1 - 2 * (m % 2))

    def chunk_there(m):
        return (m % 2) * 2 + m // 2

    def plane_device(m, q):
        return (z + q - 2 * z * q) * 32 + ((g + offset_of(m)) % 4) * g_step + h * h_step + c

    def served_device(place):
        return z * 32 + g * g_step + (place // 2) * h_step + place % 2

    def source_device(source):
        kind, far = source // 4, source % 4
        return z * 32 + (1 - kind) * (y * 8 + far * 2) + kind * (far * 8 + x * 2 + 1)

    def place_there(source):
        kind = source // 4
        return ((1 - kind) * x + kind * y) * 2 + c

    def rows_of(index):
        return pl.ds(pl.multiple_of(index * slot_rows, slot_rows), slot_rows)

    barrier = pltpu.get_barrier_semaphore()

    def greet(device):
        pl.semaphore_signal(barrier, inc=1, device_id=device, device_id_type=MESH)

    for i in range(1, NEAR):
        greet((dp, plane_device(i // 2, i % 2)))

    def greet_sets(k, carry):
        greet((dp, served_device((my_place + k) % NEAR)))
        greet((dp, source_device((my_source + k) % NEAR)))
        return carry

    lax.fori_loop(1, NEAR, greet_sets, 0)
    greet((1 - dp, me))

    weights = [
        pltpu.make_async_copy(wg_hbm.at[0], wg, w_sem.at[0]),
        pltpu.make_async_copy(wu_hbm.at[0], wu, w_sem.at[1]),
        pltpu.make_async_copy(wd_hbm.at[0], wd, w_sem.at[2]),
    ]
    for copy in weights:
        copy.start()

    gathered[0, 0:rows, :] = tokens_ref[...]
    pl.semaphore_wait(barrier, 3 * (NEAR - 1) + 1)

    def axis_copy(m):
        slot = chunk_there(m)
        return pltpu.make_async_remote_copy(
            src_ref=tokens_ref,
            dst_ref=gathered.at[slot, pl.ds(0, rows)],
            send_sem=g_send.at[m * 2],
            recv_sem=g_recv.at[slot * 2],
            device_id=(dp, plane_device(m, 0)),
            device_id_type=MESH,
        )

    def peer_copy(m):
        return pltpu.make_async_remote_copy(
            src_ref=gathered.at[m, pl.ds(0, rows)],
            dst_ref=gathered.at[m, pl.ds(rows, rows)],
            send_sem=g_send.at[m * 2 + 1],
            recv_sem=g_recv.at[m * 2 + 1],
            device_id=(dp, plane_device(0, 1)),
            device_id_type=MESH,
        )

    def route_copy(i):
        m, q = i // 2, i % 2
        slot = chunk_there(m)
        return pltpu.make_async_remote_copy(
            src_ref=route,
            dst_ref=routes.at[slot, q],
            send_sem=r_send.at[i],
            recv_sem=r_recv.at[slot * 2 + q],
            device_id=(dp, plane_device(m, q)),
            device_id_type=MESH,
        )

    peer_copy(0).start()
    for m in range(1, 4):
        axis_copy(m).start()

    logits = lax.dot_general(
        router_ref[...], tokens_ref[...], (((1,), (1,)), ((), ())), preferred_element_type=f32
    )
    expert_row = lax.broadcasted_iota(jnp.int32, (experts, rows), 0)
    chosen = jnp.zeros((experts, rows), f32)
    for k in range(top):
        chosen = jnp.where(ids_ref[k : k + 1, :] == expert_row, 1.0, chosen)
    affinity = jnp.where(chosen > 0, 1.0 / (1.0 + jnp.exp(-logits)), 0.0)
    gates = 2.5 * affinity / jnp.sum(affinity, axis=0, keepdims=True)
    earlier = lax.broadcasted_iota(jnp.int32, (rows, rows), 0)
    later = lax.broadcasted_iota(jnp.int32, (rows, rows), 1)
    upto = jnp.where(earlier <= later, 1.0, 0.0).astype(bf16)
    ranks = jnp.dot(chosen.astype(bf16), upto, preferred_element_type=f32)
    route[...] = jnp.concatenate([chosen * ranks, gates], axis=1)
    routes[0, 0] = route[...]
    for i in range(1, NEAR):
        route_copy(i).start()

    def landed(ref, sem):
        pltpu.make_async_copy(ref, ref, sem).wait()

    def wait_tokens(m, q):
        landed(gathered.at[m, pl.ds(q * rows, rows)], g_recv.at[m * 2 + q])

    def wait_route(m, q):
        landed(routes.at[m, q], r_recv.at[m * 2 + q])

    def table(m, q):
        picked = [routes[m, q, pl.ds(served_device(place), 1), :] for place in range(NEAR)]
        return jnp.concatenate(picked, axis=0)

    def per_slot(values, count):
        values = jnp.broadcast_to(values[:, None, :], (NEAR, count, values.shape[1]))
        return values.reshape(NEAR * count, values.shape[2])

    def pack_block(j, w):
        m, q = CHUNKS[j][w]
        codes = per_slot(table(m, q)[:, :rows], CAP)
        slot = lax.broadcasted_iota(jnp.int32, (NEAR * CAP, rows), 0) % CAP
        select = jnp.where(codes == (slot + 1).astype(f32), 1.0, 0.0).astype(bf16)

        def tile(n, carry):
            columns = pl.ds(pl.multiple_of(n * 512, 512), 512)
            block = gathered[m, q * rows : (q + 1) * rows, columns]
            packed[j, w, :, columns] = jnp.dot(select, block, preferred_element_type=f32).astype(bf16)
            return carry

        lax.fori_loop(0, depth // 512, tile, 0)

    def weights_of(j):
        (m, q), (far_m, far_q) = CHUNKS[j]
        near, far = table(m, q), table(far_m, far_q)
        half = lax.broadcasted_iota(jnp.int32, (NEAR, 2 * rows), 1) < rows
        swap = lambda t: jnp.concatenate([t[:, rows:], t[:, :rows]], axis=1)
        codes = per_slot(jnp.where(half, near, swap(far)), slot_rows)
        gates = per_slot(jnp.where(half, swap(near), far), slot_rows)
        slot = lax.broadcasted_iota(jnp.int32, (NEAR * slot_rows, 2 * rows), 0) % slot_rows
        block = lax.broadcasted_iota(jnp.int32, (NEAR * slot_rows, 2 * rows), 1) // rows
        wanted = jnp.where(slot // CAP == block, slot % CAP + 1, -1).astype(f32)
        return jnp.where(codes == wanted, gates, 0.0)

    def hand_out(i, k):
        place = (my_place + k) % NEAR
        j, w = i // 2, i % 2
        return pltpu.make_async_remote_copy(
            src_ref=packed.at[j, w, pl.ds(pl.multiple_of(place * CAP, CAP), CAP)],
            dst_ref=served.at[j, half_rows_of(my_source, w)],
            send_sem=d_send.at[i * NEAR + k],
            recv_sem=d_recv.at[i * NEAR + my_source],
            device_id=(dp, served_device(place)),
            device_id_type=MESH,
        )

    def half_rows_of(index, w):
        return pl.ds(pl.multiple_of(index * slot_rows + w * CAP, CAP), CAP)

    def pack_and_send(j, w):
        m, q = CHUNKS[j][w]
        if (m, q) != (0, 0):
            wait_tokens(m, q)
            wait_route(m, q)
        if (m, q) in FORWARD:
            peer_copy(FORWARD[m, q]).start()
        pack_block(j, w)
        i = j * 2 + w

        def send(k, carry):
            hand_out(i, k).start()
            return carry

        lax.fori_loop(1, NEAR, send, 0)
        pltpu.make_async_copy(
            packed.at[j, w, pl.ds(pl.multiple_of(my_place * CAP, CAP), CAP)],
            served.at[j, half_rows_of(my_source, w)],
            d_recv.at[i * NEAR + my_source],
        ).start()

    def part_of(part):
        first, last = PARTS[part]
        return pl.ds(first * 512, (last - first) * 512)

    def hand_back(m, k, part):
        source = (my_source + k) % NEAR
        place = place_there(source)
        return pltpu.make_async_remote_copy(
            src_ref=served.at[m, rows_of(source), part_of(part)],
            dst_ref=back.at[m, rows_of(place), part_of(part)],
            send_sem=t_send.at[(m * 2 + part) * NEAR + k],
            recv_sem=t_recv.at[(m * 2 + part) * NEAR + place],
            device_id=(dp, source_device(source)),
            device_id_type=MESH,
        )

    def serve(m, carry):
        def arrive(source, carry):
            landed(served.at[m, half_rows_of(source, 0)], d_recv.at[m * 2 * NEAR + source])
            landed(served.at[m, half_rows_of(source, 1)], d_recv.at[(m * 2 + 1) * NEAR + source])
            return carry

        lax.fori_loop(0, NEAR, arrive, 0)

        def into_hidden(n, carry):
            columns = pl.ds(pl.multiple_of(n * 256, 256), 256)
            gate_part = jnp.dot(served[m], wg[:, columns], preferred_element_type=f32)
            up_part = jnp.dot(served[m], wu[:, columns], preferred_element_type=f32)
            act = gate_part / (1.0 + jnp.exp(-gate_part)) * up_part
            hidden[:, columns] = act.astype(bf16)
            return carry

        lax.fori_loop(0, width // 256, into_hidden, 0)

        def out_of_hidden(n, carry):
            columns = pl.ds(pl.multiple_of(n * 512, 512), 512)
            served[m, :, columns] = jnp.dot(
                hidden[...], wd[:, columns], preferred_element_type=f32
            ).astype(bf16)
            return carry

        for part, (first, last) in enumerate(PARTS):
            lax.fori_loop(first, last, out_of_hidden, 0)

            def send(k, carry, part=part):
                hand_back(m, k, part).start()
                return carry

            lax.fori_loop(1, NEAR, send, 0)
            pltpu.make_async_copy(
                served.at[m, rows_of(my_source), part_of(part)],
                back.at[m, rows_of(my_place), part_of(part)],
                t_recv.at[(m * 2 + part) * NEAR + my_place],
            ).start()
        return carry

    def sum_copy(m, q):
        slot = chunk_there(m)
        return pltpu.make_async_remote_copy(
            src_ref=gathered.at[m, pl.ds(q * rows, rows)],
            dst_ref=sums.at[slot * 2 + q],
            send_sem=p_send.at[m * 2 + q],
            recv_sem=p_recv.at[slot * 2 + q],
            device_id=(dp, plane_device(m, q)),
            device_id_type=MESH,
        )

    def peer_sum_copy(m):
        return pltpu.make_async_remote_copy(
            src_ref=gathered.at[m, pl.ds(rows, rows)],
            dst_ref=sums.at[m * 2 + 1],
            send_sem=p_send.at[m * 2 + 1],
            recv_sem=p_recv.at[m * 2 + 1],
            device_id=(dp, plane_device(0, 1)),
            device_id_type=MESH,
        )

    def last_copy(part):
        return pltpu.make_async_remote_copy(
            src_ref=gathered.at[3, pl.ds(rows, rows), part_of(part)],
            dst_ref=sums.at[7, pl.ds(0, rows), part_of(part)],
            send_sem=l_send.at[part],
            recv_sem=l_recv.at[part],
            device_id=(dp, plane_device(3, 1)),
            device_id_type=MESH,
        )

    def combine(j):
        (m, q), (far_m, far_q) = CHUNKS[j]

        def arrive(part):
            def one(place, carry):
                landed(
                    back.at[j, rows_of(place), part_of(part)],
                    t_recv.at[(j * 2 + part) * NEAR + place],
                )
                return carry

            lax.fori_loop(0, NEAR, one, 0)

        for place, other in CHUNKS[j]:
            if other == 0:
                peer_copy(place).wait_send()
        weight = weights_of(j).T
        high = weight.astype(bf16)
        low = (weight - high.astype(f32)).astype(bf16)

        def tile(n, carry):
            columns = pl.ds(pl.multiple_of(n * 512, 512), 512)
            block = back[j, :, columns]
            total = jnp.dot(high, block, preferred_element_type=f32)
            total = (total + jnp.dot(low, block, preferred_element_type=f32)).astype(bf16)
            gathered[m, q * rows : (q + 1) * rows, columns] = total[:rows]
            gathered[far_m, far_q * rows : (far_q + 1) * rows, columns] = total[rows:]
            return carry

        for part, (first, last) in enumerate(PARTS):
            arrive(part)
            lax.fori_loop(first, last, tile, 0)
            if j == 3:
                last_copy(part).start()
        for place, other in CHUNKS[j]:
            if place in VIA_PEER:
                if other == 1:
                    peer_sum_copy(place).start()
            elif (place, other) not in ((0, 0), (3, 1)):
                sum_copy(place, other).start()

    def pass_on(m):
        landed(sums.at[m * 2 + 1], p_recv.at[m * 2 + 1])

        def tile(n, carry):
            columns = pl.ds(pl.multiple_of(n * 512, 512), 512)
            both = gathered[m, 0:rows, columns].astype(f32) + sums[m * 2 + 1, :, columns].astype(f32)
            gathered[m, 0:rows, columns] = both.astype(bf16)
            return carry

        lax.fori_loop(0, depth // 512, tile, 0)
        sum_copy(m, 0).start()

    def serve_chunk(m):
        lax.fori_loop(m, m + 1, serve, 0)

    for j, w in ((3, 0), (0, 0), (0, 1), (2, 0), (1, 0), (1, 1)):
        pack_and_send(j, w)
    for copy in weights:
        copy.wait()
    serve_chunk(0)
    pack_and_send(2, 1)
    serve_chunk(1)
    pack_and_send(3, 1)
    combine(0)
    serve_chunk(2)
    combine(1)
    serve_chunk(3)
    combine(2)
    pass_on(1)

    plane = jnp.zeros((experts, 2 * rows), f32)
    for i in range(NEAR):
        plane = plane + jnp.where(routes[i // 2, i % 2] > 0, 1.0, 0.0)
    ones = jnp.where(lax.broadcasted_iota(jnp.int32, (8, 2 * rows), 1) < rows, 1.0, 0.0).astype(bf16)
    tally[...] = jnp.zeros_like(tally)
    tally[:, 0:experts] = lax.dot_general(
        ones, plane.astype(bf16), (((1,), (1,)), ((), ())), preferred_element_type=f32
    )

    def tally_copy(k):
        return pltpu.make_async_remote_copy(
            src_ref=tally,
            dst_ref=tallies.at[my_source],
            send_sem=c_send.at[k],
            recv_sem=c_recv.at[my_source],
            device_id=(dp, served_device((my_place + k) % NEAR)),
            device_id_type=MESH,
        )

    def send_tally(k, carry):
        tally_copy(k).start()
        return carry

    lax.fori_loop(1, NEAR, send_tally, 0)
    pltpu.make_async_copy(tally, tallies.at[my_source], c_recv.at[my_source]).start()


    group = jnp.zeros((8, 2 * experts), f32)
    for source in range(NEAR):
        landed(tallies.at[source], c_recv.at[source])
        group = group + tallies[source]
    twin[0] = group
    twin_copy = pltpu.make_async_remote_copy(
        src_ref=twin.at[0],
        dst_ref=twin.at[1],
        send_sem=x_send,
        recv_sem=x_recv,
        device_id=(1 - dp, me),
        device_id_type=MESH,
    )
    twin_copy.start()

    combine(3)
    pass_on(2)

    twin_copy.wait()
    load_ref[...] = (twin[0, 0:1, 0:experts] + twin[1, 0:1, 0:experts]) * (1.0 / 1024.0)

    for m in range(1, 4):
        axis_copy(m).wait_send()
    for i in range(1, NEAR):
        route_copy(i).wait_send()

    def sent(k, carry):
        tally_copy(k).wait_send()

        def sent_chunk(m, carry):
            hand_out(m * 2, k).wait_send()
            hand_out(m * 2 + 1, k).wait_send()
            hand_back(m, k, 0).wait_send()
            hand_back(m, k, 1).wait_send()
            return carry

        return lax.fori_loop(0, 4, sent_chunk, carry)

    lax.fori_loop(1, NEAR, sent, 0)

    early, late = [1, 4, 6], [2, 7]
    for i in early:
        landed(sums.at[i], p_recv.at[i])

    def gather_early(n, carry):
        columns = pl.ds(pl.multiple_of(n * 512, 512), 512)
        total = gathered[0, 0:rows, columns].astype(f32)
        for i in early:
            total = total + sums[i, :, columns].astype(f32)
        so_far[:, columns] = total
        return carry

    lax.fori_loop(0, depth // 512, gather_early, 0)
    landed(sums.at[2], p_recv.at[2])
    for part in range(2):
        landed(sums.at[7, pl.ds(0, rows), part_of(part)], l_recv.at[part])

    def finish(n, carry):
        columns = pl.ds(pl.multiple_of(n * 512, 512), 512)
        total = so_far[:, columns]
        for i in late:
            total = total + sums[i, :, columns].astype(f32)
        mixed_ref[:, columns] = total.astype(bf16)
        return carry

    lax.fori_loop(0, depth // 512, finish, 0)
    sum_copy(0, 1).wait_send()
    for m in range(1, 4):
        sum_copy(m, 0).wait_send()
        if m in VIA_PEER:
            peer_sum_copy(m).wait_send()
        else:
            last_copy(0).wait_send()
            last_copy(1).wait_send()


def local(tokens, expert_ids, router_weight, gate_weight, up_weight, down_weight):
    rows, depth = tokens.shape
    top = expert_ids.shape[1]
    experts = router_weight.shape[1]
    width = gate_weight.shape[2]
    bf16, f32 = jnp.bfloat16, jnp.float32
    slots = NEAR * 2 * CAP
    vmem = pl.BlockSpec(memory_space=pltpu.VMEM)
    hbm = pl.BlockSpec(memory_space=pl.ANY)
    dma = pltpu.SemaphoreType.DMA
    mixed, load = pl.pallas_call(
        functools.partial(moe_kernel, (rows, depth, width, experts, top)),
        out_shape=(
            jax.ShapeDtypeStruct((rows, depth), bf16),
            jax.ShapeDtypeStruct((1, experts), f32),
        ),
        in_specs=[vmem, vmem, vmem, hbm, hbm, hbm],
        out_specs=(vmem, vmem),
        scratch_shapes=[
            pltpu.VMEM((depth, width), bf16),
            pltpu.VMEM((depth, width), bf16),
            pltpu.VMEM((width, depth), bf16),
            pltpu.VMEM((4, 2 * rows, depth), bf16),
            pltpu.VMEM((4, 2, experts, 2 * rows), f32),
            pltpu.VMEM((4, 2, NEAR * CAP, depth), bf16),
            pltpu.VMEM((4, slots, depth), bf16),
            pltpu.VMEM((4, slots, depth), bf16),
            pltpu.VMEM((NEAR, rows, depth), bf16),
            pltpu.VMEM((rows, depth), f32),
            pltpu.VMEM((slots, width), bf16),
            pltpu.VMEM((experts, 2 * rows), f32),
            pltpu.VMEM((8, 2 * experts), f32),
            pltpu.VMEM((NEAR, 8, 2 * experts), f32),
            pltpu.VMEM((2, 8, 2 * experts), f32),
            dma((3,)),
            dma((NEAR,)), dma((NEAR,)),
            dma((NEAR,)), dma((NEAR,)),
            dma((8 * NEAR,)), dma((8 * NEAR,)),
            dma((8 * NEAR,)), dma((8 * NEAR,)),
            dma((NEAR,)), dma((NEAR,)),
            dma((NEAR,)), dma((NEAR,)),
            dma, dma,
            dma((2,)), dma((2,)),
        ],
        compiler_params=pltpu.CompilerParams(
            collective_id=0, has_side_effects=True, vmem_limit_bytes=60 * 1024 * 1024
        ),
    )(tokens, expert_ids.T, router_weight.T, gate_weight, up_weight, down_weight)
    return mixed, load.reshape(experts)


def solution(mesh):
    return jax.shard_map(
        local,
        mesh=mesh,
        in_specs=(
            P(("dp", "expert"), None),
            P(("dp", "expert"), None),
            P(),
            P("expert", None, None),
            P("expert", None, None),
            P("expert", None, None),
        ),
        out_specs=(P(("dp", "expert"), None), P()),
        check_vma=False,
    )
```
